256 devices in a mesh: slab: 16 (over x, y_lo, core), dom: 16 (over z, y_hi).
Axes of the slice: x: 4, y: 4 (y_hi: 2, y_lo: 2; y = y_hi * 2 + y_lo), z: 8, core: 2. Of those that a mesh axis runs over, the one named last changes fastest.
Arguments:
- rhs: float32 [6, 16, 24576], P(None, 'slab', 'dom'), may hold values from -6 to 6
- dshift: float32 [16, 24576], P('slab', 'dom'), may hold values from 0.5 to 4
- stiff: bfloat16 [16, 4096, 9216], P('slab', 'dom'), may hold values from -0.15625 to 0.15625
- face_k: bfloat16 [16, 2, 64, 9216], P('slab', None, 'dom'), may hold values from -0.625 to 0.625
- elem_col: int32 [16, 4096], P('slab', 'dom'), may hold values from 0 to 15
- elem_row: int32 [16, 4096], P('slab', 'dom'), may hold values from 0 to 255
- face_rows: int32 [16, 2], P('slab'), may hold values from 96 to 384, as said below
Outputs:
- solution: float32 [6, 16, 24576], P(None, 'slab', 'dom')
- residual: float32 [6, 16, 24576], P(None, 'slab', 'dom')
The draws below stay inside these ranges and needn't reach their ends.
Inputs may be any that keep to these rules, and one draw needn't show every extreme that they name: `face_rows`: in every draw one slab has a lower face with all 384 rows live.
All inputs are finite; a program needn't handle non-finite values.
Results may differ from the reference program's by a relative error of at most 0.0003.
Values sent between devices are 32-bit elements; how exact they have to be, the bound alone decides.
No kernel may reach another device: no remote copies, remote signals or barrier semaphores. Data moves between devices by JAX's collectives and lax.ppermute only.
A program may use at most 64 MiB of HBM per device.

```python
import math
import jax
import jax.numpy as jnp
from jax import lax

BLOCK = 96
CASES = 6
ITERS = 2
RB_DEV = 16
EB_DEV = 256
FB_DEV = 4
SLAB_BLOCKS = 256
FACE_ROWS = 384
N_SLAB = 16
N_DOM = 16


def draw_face_rows(key, part):
    counts = jax.random.randint(key, (N_SLAB, 2), FACE_ROWS // 4, FACE_ROWS + 1)
    chosen = jax.random.randint(jax.random.fold_in(key, 7), (), 0, N_SLAB)
    return counts.at[chosen, 0].set(FACE_ROWS).astype(jnp.int32)


def set_ends(drawn, stream_key, least, top_value):
    index_at = [jax.random.randint(jax.random.fold_in(stream_key, axis), (), 0, length) for axis, length in enumerate(drawn.shape)]
    widest = drawn.shape.index(max(drawn.shape))
    beside = index_at[:widest] + [(index_at[widest] + 1) % drawn.shape[widest]] + index_at[widest + 1:]
    return drawn.at[tuple(index_at)].set(least).at[tuple(beside)].set(top_value)


def levels(own_key, shape, shards, least, high):
    loudness, own = 1.0, jax.random.fold_in(own_key, 6)
    for position, shards_of in shards:
        draws = jnp.exp(jax.random.uniform(jax.random.fold_in(own, position), (shards_of,), jnp.float32, least / len(shards), high / len(shards)))
        loudness = loudness * jnp.repeat(draws, shape[position] // shards_of).reshape([-1 if axis == position else 1 for axis in range(len(shape))])
    return loudness


def gaussian(rng, dims, scale, reach, split=(), held_as=jnp.bfloat16):
    drawn = scale * jax.random.normal(rng, dims, jnp.float32)
    if split:
        drawn = drawn * levels(rng, dims, split, -0.22, 0.18)
    return jnp.clip(drawn, -reach, reach).astype(held_as)


def setup_inputs(seed: int = 0) -> dict:
    arg_keys = jax.random.split(jax.random.key(seed), 8)
    rhs = gaussian(arg_keys[0], (CASES, N_SLAB, SLAB_BLOCKS * BLOCK), 1.0, 6.0, ((1, 16), (2, 16)), jnp.float32)
    dshift = jnp.clip(jnp.exp(math.log(4.0) - 2.0794415 * jax.random.uniform(arg_keys[1], (N_SLAB, SLAB_BLOCKS * BLOCK), jnp.float32) ** levels(arg_keys[1], (N_SLAB, SLAB_BLOCKS * BLOCK), ((0, 16), (1, 16)), -0.2, 0.2)), 0.5, 4.0)
    stiff = gaussian(arg_keys[2], (N_SLAB, N_DOM * EB_DEV, BLOCK * BLOCK), (BLOCK * EB_DEV // RB_DEV) ** -0.5, 0.15625, ((0, 16), (1, 16)))
    face_k = gaussian(arg_keys[3], (N_SLAB, 2, N_DOM * FB_DEV, BLOCK * BLOCK), BLOCK ** -0.5, 0.625, ((0, 16), (2, 16)))
    elem_col = set_ends(jax.random.randint(arg_keys[4], (N_SLAB, N_DOM * EB_DEV), 0, RB_DEV), jax.random.fold_in(arg_keys[4], 1), 0, RB_DEV - 1).astype(jnp.int32)
    elem_row = set_ends(jax.random.randint(arg_keys[5], (N_SLAB, N_DOM * EB_DEV), 0, SLAB_BLOCKS), jax.random.fold_in(arg_keys[5], 1), 0, SLAB_BLOCKS - 1).astype(jnp.int32)
    face_rows = draw_face_rows(jax.random.fold_in(arg_keys[7], 71), 0)
    return {"rhs": rhs, "dshift": dshift, "stiff": stiff, "face_k": face_k, "elem_col": elem_col, "elem_row": elem_row, "face_rows": face_rows}


highest = lax.Precision.HIGHEST


def slab_views(vector):
    leading = vector.shape[0]
    span = RB_DEV * BLOCK
    shaped = vector.reshape(leading, N_SLAB, N_DOM, span)
    lower = shaped[..., :FACE_ROWS].reshape(leading, N_SLAB, N_DOM, FB_DEV, BLOCK)
    upper = shaped[..., span - FACE_ROWS:].reshape(leading, N_SLAB, N_DOM, FB_DEV, BLOCK)
    return lower, upper


def add_faces(vector, lower_add, upper_add):
    leading = vector.shape[0]
    span = RB_DEV * BLOCK
    shaped = vector.reshape(leading, N_SLAB, N_DOM, span)
    shaped = shaped.at[..., :FACE_ROWS].add(lower_add.reshape(leading, N_SLAB, N_DOM, FACE_ROWS))
    shaped = shaped.at[..., span - FACE_ROWS:].add(upper_add.reshape(leading, N_SLAB, N_DOM, FACE_ROWS))
    return shaped.reshape(leading, N_SLAB, SLAB_BLOCKS * BLOCK)


def reference(rhs, dshift, stiff, face_k, elem_col, elem_row, face_rows):
    owner_base = (jnp.arange(N_DOM * EB_DEV, dtype=jnp.int32) // EB_DEV) * RB_DEV
    glob_cols = (elem_col + owner_base[None, :]).astype(jnp.int32)
    positions = jnp.arange(FACE_ROWS, dtype=jnp.int32)
    masks = (positions[None, None, :] < face_rows[:, :, None]).astype(jnp.float32)
    mask_low = masks[:, 0].reshape(1, N_SLAB, 1, FB_DEV, BLOCK)
    mask_up = masks[:, 1].reshape(1, N_SLAB, 1, FB_DEV, BLOCK)
    kface = face_k.astype(jnp.float32).reshape(N_SLAB, 2, N_DOM, FB_DEV, BLOCK, BLOCK)
    k_low = kface[:, 0]
    k_up = kface[:, 1]

    def intra_forward(items):
        blocks, columns, targets, vector = items
        matrices = blocks.astype(jnp.float32).reshape(-1, BLOCK, BLOCK)
        picked = vector.reshape(CASES, SLAB_BLOCKS, BLOCK)[:, columns]
        terms = jnp.einsum("gab,cgb->cga", matrices, picked, precision=highest)
        summed = jnp.zeros((CASES, SLAB_BLOCKS, BLOCK), jnp.float32).at[:, targets].add(terms)
        return summed.reshape(CASES, SLAB_BLOCKS * BLOCK)

    def intra_adjoint(items):
        blocks, columns, targets, vector = items
        matrices = blocks.astype(jnp.float32).reshape(-1, BLOCK, BLOCK)
        picked = vector.reshape(CASES, SLAB_BLOCKS, BLOCK)[:, targets]
        terms = jnp.einsum("gab,cga->cgb", matrices, picked, precision=highest)
        summed = jnp.zeros((CASES, SLAB_BLOCKS, BLOCK), jnp.float32).at[:, columns].add(terms)
        return summed.reshape(CASES, SLAB_BLOCKS * BLOCK)

    def per_slab(function, vector):
        result = lax.map(function, (stiff, glob_cols, elem_row, jnp.moveaxis(vector, 1, 0)))
        return jnp.moveaxis(result, 0, 1)

    def apply_operator(vector):
        lower, upper = slab_views(vector)
        from_below = jnp.roll(upper, 1, axis=1)
        from_above = jnp.roll(lower, -1, axis=1)
        term_low = jnp.einsum("sdiab,csdib->csdia", k_low, from_below, precision=highest) * mask_low
        term_up = jnp.einsum("sdiab,csdib->csdia", k_up, from_above, precision=highest) * mask_up
        image = add_faces(per_slab(intra_forward, vector), term_low, term_up)
        low_rows, up_rows = slab_views(image)
        back_low = jnp.einsum("sdiab,csdia->csdib", k_low, low_rows * mask_low, precision=highest)
        back_up = jnp.einsum("sdiab,csdia->csdib", k_up, up_rows * mask_up, precision=highest)
        adjoint = add_faces(per_slab(intra_adjoint, image), jnp.roll(back_up, 1, axis=1), jnp.roll(back_low, -1, axis=1))
        return dshift[None] * vector + adjoint

    def column_squares(items):
        blocks, columns = items
        matrices = blocks.astype(jnp.float32).reshape(-1, BLOCK, BLOCK)
        squares = jnp.sum(matrices * matrices, axis=1)
        summed = jnp.zeros((SLAB_BLOCKS, BLOCK), jnp.float32).at[columns].add(squares)
        return summed.reshape(SLAB_BLOCKS * BLOCK)

    inner = lax.map(column_squares, (stiff, glob_cols))
    sq_low = jnp.sum(k_low * k_low * mask_low[0][..., None], axis=3)
    sq_up = jnp.sum(k_up * k_up * mask_up[0][..., None], axis=3)
    diag_terms = add_faces(inner[None], jnp.roll(sq_up, 1, axis=0)[None], jnp.roll(sq_low, -1, axis=0)[None])
    inverse = 1.0 / (dshift[None] + diag_terms)

    def inner_product(first, second):
        return jnp.sum(first * second, axis=(1, 2))

    residual = rhs
    precond = inverse * residual
    direction = precond
    solution = jnp.zeros_like(rhs)
    rz_now = inner_product(residual, precond)
    for sweep in range(ITERS):
        image = apply_operator(direction)
        step_size = rz_now / inner_product(direction, image)
        solution = solution + step_size[:, None, None] * direction
        residual = residual - step_size[:, None, None] * image
        if sweep + 1 < ITERS:
            precond = inverse * residual
            rz_next = inner_product(residual, precond)
            direction = precond + (rz_next / rz_now)[:, None, None] * direction
            rz_now = rz_next
    return solution, residual
```

```python
import jax
import jax.numpy as jnp
from jax import lax
from jax.experimental import pallas as pl
from jax.experimental.pallas import tpu as pltpu
from jax.sharding import Mesh
from jax.sharding import PartitionSpec as P

BLOCK = 96
CASES = 6
DOM = ("dom_0", "dom_1")
SLAB = ("slab_0", "slab_1", "slab_2")
F32 = jnp.float32
BF16 = jnp.bfloat16
LANES = 128
OWN = 16
STORED = 256
SLAB_ROWS = 256
GROUP = 32
STEPS = STORED // GROUP
CHUNK = 72
TILES = 12
FACE = 4
MIB = 1024 * 1024


def lane(rows):
    return lax.broadcasted_iota(jnp.int32, (rows, LANES), 1)


def spread(t0, t1, t2):
    at = lane(t0.shape[0])
    v0 = t0
    v1 = jnp.where(at < 32, pltpu.roll(t0, 32, 1), pltpu.roll(t1, 32, 1))
    v2 = jnp.where(at < 64, pltpu.roll(t1, 64, 1), pltpu.roll(t2, 64, 1))
    v3 = pltpu.roll(t2, 96, 1)
    return [jnp.where(at < BLOCK, v, 0.0) for v in (v0, v1, v2, v3)]


def packed(v0, v1, v2, v3):
    at = lane(v0.shape[0])
    r1 = pltpu.roll(v1, 96, 1)
    r2 = pltpu.roll(v2, 64, 1)
    r3 = pltpu.roll(v3, 32, 1)
    return (
        jnp.where(at < 96, v0, r1),
        jnp.where(at < 64, r1, r2),
        jnp.where(at < 32, r2, r3),
    )


def halves(v):
    high = v.astype(BF16).astype(F32)
    return jnp.concatenate([high, v - high], axis=0).astype(BF16)


def rows_live(shape, dim, live, block):
    at = lax.broadcasted_iota(jnp.int32, shape, dim)
    row = 4 * (at % 24) + at // 24
    return row + block * BLOCK < live


def eight(ref, start):
    if start + 8 <= ref.shape[0]:
        return ref[start : start + 8, :]
    return pltpu.roll(ref[start - 2 : start + 6, :], 6, 0)


def block_of(held, first, stride):
    parts = [held[pl.ds(first + k * (stride // 3), 24, stride=stride), :] for k in range(3)]
    return jnp.concatenate(spread(*parts), axis=0)


def face_prep(live_ref, x_ref, k_ref, sq_ref, held):
    for t in range(CHUNK):
        held[t * 8 : (t + 1) * 8, :] = x_ref[:, t * LANES : (t + 1) * LANES]
    for k in range(2):
        sums = []
        for i in range(FACE):
            whole = block_of(held, k * FACE + i, 24)
            k_ref[k * FACE + i] = whole.astype(BF16)
            masked = jnp.where(rows_live((BLOCK, LANES), 0, live_ref[k], i), whole, 0.0)
            total = jnp.sum(masked * masked, axis=0, keepdims=True)
            sums.append(jnp.broadcast_to(total, (8, LANES)))
        for t, tile in enumerate(packed(*sums)):
            sq_ref[k, :, t * LANES : (t + 1) * LANES] = tile


def stiff_prep(col_ref, x_ref, k_ref, diag_ref, held, acc):
    step = pl.program_id(0)

    @pl.when(step == 0)
    def _():
        acc[...] = jnp.zeros_like(acc)

    for half in range(GROUP // 16):
        for t in range(CHUNK):
            held[t * 16 : (t + 1) * 16, :] = x_ref[
                half * 16 : (half + 1) * 16, t * LANES : (t + 1) * LANES
            ].astype(F32)
        for e in range(16):
            whole = block_of(held, e, 48)
            k_ref[half * 16 + e] = whole.astype(BF16)
            total = jnp.sum((whole * whole).reshape(12, 8, LANES), axis=0)
            j = col_ref[step * GROUP + half * 16 + e]
            acc[j] = acc[j] + total

    @pl.when(step == STEPS - 1)
    def _():
        for q in range(OWN // 4):
            sums = [
                jnp.broadcast_to(jnp.sum(acc[q * 4 + i], axis=0, keepdims=True), (8, LANES))
                for i in range(4)
            ]
            for t, tile in enumerate(packed(*sums)):
                at = (q * 3 + t) * LANES
                diag_ref[:, at : at + LANES] = tile


def forward(col_ref, row_ref, v_ref, k_ref, out_ref, cols, acc):
    step = pl.program_id(0)

    @pl.when(step == 0)
    def _():
        acc[...] = jnp.zeros_like(acc)
        for q in range(OWN // 4):
            tiles = [v_ref[:, (q * 3 + t) * LANES : (q * 3 + t + 1) * LANES] for t in range(3)]
            for i, v in enumerate(spread(*tiles)):
                cols[q * 4 + i] = halves(v)

    for first in range(0, GROUP, 8):
        terms = []
        for e in range(first, first + 8):
            x = cols[col_ref[step * GROUP + e]]
            out = lax.dot_general(
                x, k_ref[e], (((1,), (1,)), ((), ())), preferred_element_type=F32
            )
            terms.append(out[:8] + out[8:])
        for e in range(first, first + 8):
            r = row_ref[step * GROUP + e]
            acc[r, :, :BLOCK] = acc[r, :, :BLOCK] + terms[e - first]

    @pl.when(step == STEPS - 1)
    def _():
        for g in range(SLAB_ROWS // 4):
            for t, tile in enumerate(packed(*[acc[g * 4 + i] for i in range(4)])):
                at = (g // 4) * CHUNK + ((g % 4) * 3 + t) * CASES
                out_ref[at : at + CASES, :] = tile[:CASES]


def adjoint(
    col_ref, row_ref, y_ref, k_ref, v_ref, shift_ref, low_ref, up_ref, out_ref, rows, acc
):
    step = pl.program_id(0)

    @pl.when(step == 0)
    def _():
        acc[...] = jnp.zeros_like(acc)
        for g in range(SLAB_ROWS // 4):
            at = (g // 4) * CHUNK + (g % 4) * 3 * CASES
            tiles = [eight(y_ref, at + t * CASES) for t in range(3)]
            for i, v in enumerate(spread(*tiles)):
                rows[g * 4 + i] = halves(v)

    for first in range(0, GROUP, 8):
        terms = []
        for e in range(first, first + 8):
            y = rows[row_ref[step * GROUP + e]]
            out = jnp.dot(y[:, :BLOCK], k_ref[e], preferred_element_type=F32)
            terms.append(out[:8] + out[8:])
        for e in range(first, first + 8):
            j = col_ref[step * GROUP + e]
            acc[j] = acc[j] + terms[e - first]

    @pl.when(step == STEPS - 1)
    def _():
        for q in range(OWN // 4):
            for t, tile in enumerate(packed(*[acc[q * 4 + i] for i in range(4)])):
                at = (q * 3 + t) * LANES
                to = slice(at, at + LANES)
                whole = tile + shift_ref[:, to] * v_ref[:, to]
                if q == 0:
                    whole = whole + low_ref[:, to]
                if q == OWN // 4 - 1:
                    whole = whole + up_ref[:, t * LANES : (t + 1) * LANES]
                out_ref[:, to] = whole


def summed(at_ref, live_ref, y_ref, low_ref, up_ref, k_ref, out_ref):
    half = at_ref[0]
    whole = y_ref[0]
    for z in range(1, y_ref.shape[0]):
        whole = whole + y_ref[z]
    out_ref[...] = whole
    for k, face_ref in enumerate((low_ref, up_ref)):
        tiles = [face_ref[:, t * LANES : (t + 1) * LANES] for t in range(3)]
        terms = []
        for i, v in enumerate(spread(*tiles)):
            out = lax.dot_general(
                halves(v), k_ref[k * FACE + i], (((1,), (1,)), ((), ())), preferred_element_type=F32
            )
            term = out[:8] + out[8:]
            term = jnp.where(rows_live((8, BLOCK), 1, live_ref[k], i), term, 0.0)
            terms.append(jnp.concatenate([term, jnp.zeros((8, LANES - BLOCK), F32)], axis=1))
        for t, tile in enumerate(packed(*terms)):
            for h in range(2):
                at = h * CHUNK + (k * 9 + t) * CASES
                added = jnp.where(half == h, tile[:CASES], 0.0)
                out_ref[at : at + CASES, :] = out_ref[at : at + CASES, :] + added


def finished(at_ref, live_ref, a_ref, b_ref, k_ref, out_ref, back_ref, square_ref, held):
    half = at_ref[0]
    both = a_ref[...] + b_ref[...]
    for z in range(out_ref.shape[0]):
        out_ref[z] = both
    own = jnp.where(half == 0, both[:CHUNK], both[CHUNK:])
    held[...] = own
    square = jnp.zeros((8, LANES), F32)
    for t in range(TILES):
        tile = eight(held, t * CASES)
        square = square + tile * tile
    square_ref[...] = square
    for k in range(2):
        tiles = [eight(held, (k * 9 + t) * CASES) for t in range(3)]
        terms = []
        for i, v in enumerate(spread(*tiles)):
            v = jnp.where(rows_live((8, LANES), 1, live_ref[k], i), v, 0.0)
            y = halves(v)
            out = jnp.dot(y[:, :BLOCK], k_ref[k * FACE + i], preferred_element_type=F32)
            terms.append(out[:8] + out[8:])
        for t, tile in enumerate(packed(*terms)):
            back_ref[k, :, t * LANES : (t + 1) * LANES] = tile


SMEM = pl.BlockSpec(memory_space=pltpu.SMEM)
VMEM = pl.BlockSpec(memory_space=pltpu.VMEM)
GIVEN = pltpu.CompilerParams(vmem_limit_bytes=24 * MIB)


def shaped(*shape, dtype=F32):
    return jax.ShapeDtypeStruct(shape, dtype)


def whole_block(*shape):
    return pl.BlockSpec(shape, lambda i, *_: (0,) * len(shape))


def per_step(scalars, ins, outs, out_shape, scratch, kernel):
    return pl.pallas_call(
        kernel,
        grid_spec=pltpu.PrefetchScalarGridSpec(
            num_scalar_prefetch=scalars,
            grid=(STEPS,),
            in_specs=ins,
            out_specs=outs,
            scratch_shapes=scratch,
        ),
        out_shape=out_shape,
        compiler_params=GIVEN,
    )


BLOCKS = pl.BlockSpec((GROUP, BLOCK, LANES), lambda i, *_: (i, 0, 0))


def padded(value):
    return jnp.pad(value, ((0, 2), (0, 0)))


def body(rhs, dshift, stiff, face_k, elem_col, elem_row, face_rows):
    span = rhs.shape[2]
    face_len = FACE * BLOCK
    columns, targets = elem_col[0], elem_row[0]
    live = face_rows[0]
    half = lax.axis_index("dom_1").astype(jnp.int32).reshape(1)
    z_count = lax.axis_size("dom_0")
    slabs = lax.axis_size(SLAB)
    up = [(i, (i + 1) % slabs) for i in range(slabs)]
    down = [(b, a) for a, b in up]

    def to_above(value):
        return lax.ppermute(value, SLAB, up)

    def to_below(value):
        return lax.ppermute(value, SLAB, down)

    def lower(value):
        return value[:, :face_len]

    def upper(value):
        return value[:, span - face_len :]

    faces, face_sq = pl.pallas_call(
        face_prep,
        in_specs=[SMEM, VMEM],
        out_specs=(VMEM, VMEM),
        out_shape=(
            shaped(2 * FACE, BLOCK, LANES, dtype=BF16),
            shaped(2, 8, face_len),
        ),
        scratch_shapes=[pltpu.VMEM((CHUNK * 8, LANES), F32)],
        compiler_params=GIVEN,
    )(live, face_k[0].astype(F32).reshape(2 * FACE, BLOCK * BLOCK))
    sq_above = to_below(face_sq[0, :1])
    sq_below = to_above(face_sq[1, :1])

    blocks, inner = per_step(
        1,
        [pl.BlockSpec((GROUP, BLOCK * BLOCK), lambda i, *_: (i, 0))],
        (BLOCKS, whole_block(8, span)),
        (shaped(STORED, BLOCK, LANES, dtype=BF16), shaped(8, span)),
        [pltpu.VMEM((CHUNK * 16, LANES), F32), pltpu.VMEM((OWN, 8, LANES), F32)],
        stiff_prep,
    )(columns, stiff[0])
    total = dshift + inner[:1]
    total = jnp.concatenate(
        [
            lower(total) + sq_below,
            total[:, face_len : span - face_len],
            upper(total) + sq_above,
        ],
        axis=1,
    )
    inverse = 1.0 / total
    residual = padded(rhs[:, 0])
    direction = inverse * residual

    def all_rows(vector):
        from_below = to_above(upper(vector))
        from_above = to_below(lower(vector))
        parts = per_step(
            2,
            [whole_block(8, span), BLOCKS],
            whole_block(OWN * CHUNK, LANES),
            shaped(OWN * CHUNK, LANES),
            [pltpu.VMEM((OWN, 16, LANES), BF16), pltpu.VMEM((SLAB_ROWS, 8, LANES), F32)],
            forward,
        )(columns, targets, vector, blocks)
        parts = parts.reshape(z_count, 2 * CHUNK, LANES)
        arrived = lax.all_to_all(parts, "dom_0", 0, 0, tiled=True)
        mine = pl.pallas_call(
            summed,
            in_specs=[SMEM, SMEM] + [VMEM] * 4,
            out_specs=VMEM,
            out_shape=shaped(2 * CHUNK, LANES),
            compiler_params=GIVEN,
        )(half, live, arrived, from_below, from_above, faces)
        other = lax.ppermute(mine, "dom_1", [(0, 1), (1, 0)])
        copies, back, square = pl.pallas_call(
            finished,
            in_specs=[SMEM, SMEM] + [VMEM] * 3,
            out_specs=(VMEM, VMEM, VMEM),
            out_shape=(
                shaped(z_count, 2 * CHUNK, LANES),
                shaped(2, 8, face_len),
                shaped(8, LANES),
            ),
            scratch_shapes=[pltpu.VMEM((CHUNK, LANES), F32)],
            compiler_params=GIVEN,
        )(half, live, mine, other, faces)
        full = lax.all_to_all(copies, "dom_0", 0, 0, tiled=True)
        low_add = to_above(back[1])
        up_add = to_below(back[0])
        return full.reshape(OWN * CHUNK, LANES), low_add, up_add, square

    def image_of(vector, made):
        full, low_add, up_add, _ = made
        return per_step(
            2,
            [
                whole_block(OWN * CHUNK, LANES),
                BLOCKS,
                whole_block(8, span),
                whole_block(1, span),
                whole_block(8, face_len),
                whole_block(8, face_len),
            ],
            whole_block(8, span),
            shaped(8, span),
            [pltpu.VMEM((SLAB_ROWS, 16, LANES), BF16), pltpu.VMEM((OWN, 8, LANES), F32)],
            adjoint,
        )(columns, targets, full, blocks, vector, dshift, low_add, up_add)

    def inner_product(first, second):
        return jnp.sum(first[:CASES] * second[:CASES], axis=1)

    def everywhere(value, axis):
        count = lax.axis_size(axis)
        sent = jnp.broadcast_to(value[None], (count, *value.shape))
        return lax.all_to_all(sent, axis, 0, 0, tiled=True).sum(axis=0)

    image = image_of(direction, all_rows(direction))
    second = inverse * image
    made = all_rows(second)
    sums = jnp.stack(
        [
            inner_product(residual, direction),
            inner_product(direction, image),
            inner_product(image, second),
            inner_product(dshift * second, second) + jnp.sum(made[3][:CASES], axis=1),
        ]
    )
    sums = everywhere(everywhere(sums, SLAB), DOM)
    second_image = image_of(second, made)
    rz, curv, cross, last = sums[0], sums[1], sums[2], sums[3]
    step = rz / curv
    ratio = (step * step * cross - rz) / rz
    grown = 1.0 + ratio
    curv_next = grown * grown * curv - 2.0 * grown * step * cross + step * step * last
    step_next = ratio * rz / curv_next
    on_first = (step + step_next * grown)[:, None]
    on_second = (step_next * step)[:, None]
    solution = on_first * direction[:CASES] - on_second * second[:CASES]
    residual = residual[:CASES] - on_first * image[:CASES] + on_second * second_image[:CASES]
    return (solution[:, None, :], residual[:, None, :])


def solution(mesh):
    finer = Mesh(
        mesh.devices.reshape(4, 2, 2, 8, 2), ("slab_0", "slab_1", "slab_2", "dom_0", "dom_1")
    )
    placed = (
        P(None, SLAB, DOM),
        P(SLAB, DOM),
        P(SLAB, DOM, None),
        P(SLAB, None, DOM, None),
        P(SLAB, DOM),
        P(SLAB, DOM),
        P(SLAB, None),
    )
    return jax.shard_map(
        body,
        mesh=finer,
        in_specs=placed,
        out_specs=(P(None, SLAB, DOM), P(None, SLAB, DOM)),
        check_vma=False,
    )
```

```python
import functools

import jax
import jax.numpy as jnp
from jax import lax
from jax.experimental import pallas as pl
from jax.experimental.pallas import tpu as pltpu
from jax.sharding import Mesh
from jax.sharding import PartitionSpec as P

BLOCK = 96
CASES = 6
DOM = ("dom_0", "dom_1")
SLAB = ("slab_0", "slab_1", "slab_2")
F32 = jnp.float32
BF16 = jnp.bfloat16
LANES = 128
OWN = 16
STORED = 256
SLAB_ROWS = 256
GROUP = 32
STEPS = STORED // GROUP
CHUNK = 72
TILES = 12
FACE = 4
MIB = 1024 * 1024


def lane(rows):
    return lax.broadcasted_iota(jnp.int32, (rows, LANES), 1)


def spread(t0, t1, t2):
    at = lane(t0.shape[0])
    v0 = t0
    v1 = jnp.where(at < 32, pltpu.roll(t0, 32, 1), pltpu.roll(t1, 32, 1))
    v2 = jnp.where(at < 64, pltpu.roll(t1, 64, 1), pltpu.roll(t2, 64, 1))
    v3 = pltpu.roll(t2, 96, 1)
    return [jnp.where(at < BLOCK, v, 0.0) for v in (v0, v1, v2, v3)]


def packed(v0, v1, v2, v3):
    at = lane(v0.shape[0])
    r1 = pltpu.roll(v1, 96, 1)
    r2 = pltpu.roll(v2, 64, 1)
    r3 = pltpu.roll(v3, 32, 1)
    return (
        jnp.where(at < 96, v0, r1),
        jnp.where(at < 64, r1, r2),
        jnp.where(at < 32, r2, r3),
    )


def halves(v):
    high = v.astype(BF16).astype(F32)
    return jnp.concatenate([high, v - high], axis=0).astype(BF16)


def rows_live(shape, dim, live, block):
    at = lax.broadcasted_iota(jnp.int32, shape, dim)
    row = 4 * (at % 24) + at // 24
    return row + block * BLOCK < live


def eight(ref, start):
    if start + 8 <= ref.shape[0]:
        return ref[start : start + 8, :]
    return pltpu.roll(ref[start - 2 : start + 6, :], 6, 0)


def block_of(held, first, stride):
    parts = [held[pl.ds(first + k * (stride // 3), 24, stride=stride), :] for k in range(3)]
    return jnp.concatenate(spread(*parts), axis=0)


def face_prep(live_ref, x_ref, k_ref, sq_ref, held):
    for k in range(2):
        for t in range(CHUNK):
            held[t * 8 + k * FACE : t * 8 + (k + 1) * FACE, :] = x_ref[
                k, :, t * LANES : (t + 1) * LANES
            ].astype(F32)
    for k in range(2):
        sums = []
        for i in range(FACE):
            whole = block_of(held, k * FACE + i, 24)
            k_ref[k * FACE + i] = whole.astype(BF16)
            masked = jnp.where(rows_live((BLOCK, LANES), 0, live_ref[k], i), whole, 0.0)
            total = jnp.sum(masked * masked, axis=0, keepdims=True)
            sums.append(jnp.broadcast_to(total, (8, LANES)))
        for t, tile in enumerate(packed(*sums)):
            sq_ref[k, :, t * LANES : (t + 1) * LANES] = tile


def stiff_prep(col_ref, x_ref, k_ref, diag_ref, held, acc):
    step = pl.program_id(0)

    @pl.when(step == 0)
    def _():
        acc[...] = jnp.zeros_like(acc)

    for half in range(GROUP // 16):
        for t in range(CHUNK):
            held[t * 16 : (t + 1) * 16, :] = x_ref[
                half * 16 : (half + 1) * 16, t * LANES : (t + 1) * LANES
            ].astype(F32)
        for e in range(16):
            whole = block_of(held, e, 48)
            k_ref[half * 16 + e] = whole.astype(BF16)
            total = jnp.sum((whole * whole).reshape(12, 8, LANES), axis=0)
            j = col_ref[step * GROUP + half * 16 + e]
            acc[j] = acc[j] + total

    @pl.when(step == STEPS - 1)
    def _():
        for q in range(OWN // 4):
            sums = [
                jnp.broadcast_to(jnp.sum(acc[q * 4 + i], axis=0, keepdims=True), (8, LANES))
                for i in range(4)
            ]
            for t, tile in enumerate(packed(*sums)):
                diag_ref[:, tile_at(q * 3 + t)] = tile


def tile_at(t):
    return slice(t * LANES, (t + 1) * LANES)


def part(g):
    return pl.ds(g * GROUP, GROUP)


def fetch(k_any, k_ref, sems):
    for g in range(STEPS):
        pltpu.make_async_copy(k_any.at[part(g)], k_ref.at[part(g)], sems.at[g]).start()


def fetched(k_any, k_ref, sems, g):
    pltpu.make_async_copy(k_any.at[part(g)], k_ref.at[part(g)], sems.at[g]).wait()


def forward(col_ref, row_ref, tiles, k_ref, out_ref, cols, acc, wait=None):
    for q in range(OWN // 4):
        for i, v in enumerate(spread(*tiles[q * 3 : q * 3 + 3])):
            cols[q * 4 + i] = halves(v)
    acc[...] = jnp.zeros_like(acc)

    def group(g, carry):
        base = g * GROUP
        if wait is not None:
            wait(g)
        for first in range(0, GROUP, 8):
            terms = []
            for e in range(first, first + 8):
                x = cols[col_ref[base + e]]
                out = lax.dot_general(
                    x, k_ref[base + e], (((1,), (1,)), ((), ())), preferred_element_type=F32
                )
                terms.append(out[:8] + out[8:])
            for e in range(first, first + 8):
                r = row_ref[base + e]
                acc[r, :, :BLOCK] = acc[r, :, :BLOCK] + terms[e - first]
        return carry

    lax.fori_loop(0, STEPS, group, 0)
    for g in range(SLAB_ROWS // 4):
        for t, tile in enumerate(packed(*[acc[g * 4 + i] for i in range(4)])):
            at = (g // 4) * CHUNK + ((g % 4) * 3 + t) * CASES
            out_ref[at : at + CASES, :] = tile[:CASES]


def adjoint(col_ref, row_ref, y_ref, k_ref, rows, acc, wait):
    depth = y_ref.shape[0] // (OWN // 2)
    for g in range(SLAB_ROWS // 4):
        at = (g // 8) * depth + (g // 4 % 2) * CHUNK + (g % 4) * 3 * CASES
        tiles = [eight(y_ref, at + t * CASES) for t in range(3)]
        for i, v in enumerate(spread(*tiles)):
            rows[g * 4 + i] = halves(v)
    acc[...] = jnp.zeros_like(acc)

    def group(g, carry):
        base = g * GROUP
        wait(g)
        for first in range(0, GROUP, 8):
            terms = []
            for e in range(first, first + 8):
                y = rows[row_ref[base + e]]
                out = jnp.dot(y[:, :BLOCK], k_ref[base + e], preferred_element_type=F32)
                terms.append(out[:8] + out[8:])
            for e in range(first, first + 8):
                j = col_ref[base + e]
                acc[j] = acc[j] + terms[e - first]
        return carry

    lax.fori_loop(0, STEPS, group, 0)
    tiles = []
    for q in range(OWN // 4):
        tiles += packed(*[acc[q * 4 + i] for i in range(4)])
    return tiles


def both_sides(core, near_ref, far_ref):
    near = [near_ref[:, tile_at(t)] for t in range(3)]
    far = [far_ref[:, tile_at(t)] for t in range(3)]
    below = [jnp.where(core == 0, f, n) for n, f in zip(near, far)]
    above = [jnp.where(core == 0, n, f) for n, f in zip(near, far)]
    return below, above


def send_sides(core, lower, upper, near_ref, far_ref):
    for t in range(3):
        near_ref[:, tile_at(t)] = jnp.where(core == 0, upper[t], lower[t])
        far_ref[:, tile_at(t)] = jnp.where(core == 0, lower[t], upper[t])


def first_product(
    col_ref, row_ref, at_ref, rhs_ref, shift_ref, diag_ref, near_ref, far_ref, k_any,
    out_ref, inverse_ref, v_ref, near_out, far_out, held, cols, acc, k_ref, sems,
):
    fetch(k_any, k_ref, sems)
    core = at_ref[1]
    held[...] = jnp.zeros_like(held)
    for c in range(CASES):
        held[c : c + 1, :] = rhs_ref[c]
    below, above = both_sides(core, near_ref, far_ref)
    tiles = []
    for t in range(TILES):
        total = diag_ref[:, tile_at(t)] + shift_ref[:, tile_at(t)]
        if t < 3:
            total = total + below[t]
        if t >= 9:
            total = total + above[t - 9]
        inverse = 1.0 / total
        inverse_ref[:, tile_at(t)] = inverse
        tile = inverse * held[:, tile_at(t)]
        v_ref[:, tile_at(t)] = tile
        tiles.append(tile)
    send_sides(core, tiles[:3], tiles[9:], near_out, far_out)
    wait = functools.partial(fetched, k_any, k_ref, sems)
    forward(col_ref, row_ref, tiles, k_ref, out_ref, cols, acc, wait)


def image_tiles(core, tiles, v_ref, shift_ref, near_ref, far_ref):
    below, above = both_sides(core, near_ref, far_ref)
    whole = [
        tile + shift_ref[:, tile_at(t)] * v_ref[:, tile_at(t)] for t, tile in enumerate(tiles)
    ]
    return (
        [whole[t] + below[t] for t in range(3)]
        + whole[3:9]
        + [whole[t + 9] + above[t] for t in range(3)]
    )


def placed_sums(values):
    at = lane(8)
    out = jnp.zeros((8, LANES), F32)
    for n, value in values:
        out = jnp.where(at == n, jnp.sum(value, axis=1, keepdims=True), out)
    return out


def middle_product(
    col_ref, row_ref, at_ref, y_ref, rhs_ref, shift_ref, inverse_ref, v_ref, near_ref, far_ref,
    k_any, out_ref, image_ref, w_ref, sums_ref, near_out, far_out, held, rows, cols, acc,
    k_ref, sems,
):
    fetch(k_any, k_ref, sems)
    core = at_ref[1]
    wait = functools.partial(fetched, k_any, k_ref, sems)
    tiles = adjoint(col_ref, row_ref, y_ref, k_ref, rows, acc, wait)
    tiles = image_tiles(core, tiles, v_ref, shift_ref, near_ref, far_ref)
    held[...] = jnp.zeros_like(held)
    for c in range(CASES):
        held[c : c + 1, :] = rhs_ref[c]
    sums = [jnp.zeros((8, LANES), F32) for _ in range(4)]
    second = []
    for t, image in enumerate(tiles):
        image_ref[:, tile_at(t)] = image
        w = inverse_ref[:, tile_at(t)] * image
        w_ref[:, tile_at(t)] = w
        second.append(w)
        v = v_ref[:, tile_at(t)]
        sums[0] = sums[0] + held[:, tile_at(t)] * v
        sums[1] = sums[1] + v * image
        sums[2] = sums[2] + image * w
        sums[3] = sums[3] + shift_ref[:, tile_at(t)] * w * w
    sums_ref[...] = placed_sums(enumerate(sums))
    send_sides(core, second[:3], second[9:], near_out, far_out)
    forward(col_ref, row_ref, second, k_ref, out_ref, cols, acc)


def last_product(
    col_ref, row_ref, at_ref, y_ref, shift_ref, v_ref, near_ref, far_ref, k_any,
    image_ref, rows, acc, k_ref, sems,
):
    fetch(k_any, k_ref, sems)
    wait = functools.partial(fetched, k_any, k_ref, sems)
    tiles = adjoint(col_ref, row_ref, y_ref, k_ref, rows, acc, wait)
    for t, tile in enumerate(image_tiles(at_ref[1], tiles, v_ref, shift_ref, near_ref, far_ref)):
        image_ref[:, tile_at(t)] = tile


def summed(at_ref, live_ref, y_ref, near_ref, far_ref, k_ref, *rest):
    out_ref = rest[-1]
    half = at_ref[0]
    whole = y_ref[0]
    for z in range(1, y_ref.shape[0]):
        whole = whole + y_ref[z]
    out_ref[: 2 * CHUNK, :] = whole
    if len(rest) > 1:
        out_ref[2 * CHUNK :, :] = rest[0][...]
    for k, face in enumerate(both_sides(at_ref[1], near_ref, far_ref)):
        terms = []
        for i, v in enumerate(spread(*face)):
            out = lax.dot_general(
                halves(v), k_ref[k * FACE + i], (((1,), (1,)), ((), ())), preferred_element_type=F32
            )
            term = out[:8] + out[8:]
            term = jnp.where(rows_live((8, BLOCK), 1, live_ref[k], i), term, 0.0)
            terms.append(jnp.concatenate([term, jnp.zeros((8, LANES - BLOCK), F32)], axis=1))
        for t, tile in enumerate(packed(*terms)):
            for h in range(2):
                at = h * CHUNK + (k * 9 + t) * CASES
                added = jnp.where(half == h, tile[:CASES], 0.0)
                out_ref[at : at + CASES, :] = out_ref[at : at + CASES, :] + added


def finished(at_ref, live_ref, a_ref, b_ref, k_ref, out_ref, near_out, far_out, held):
    half = at_ref[0]
    both = a_ref[...] + b_ref[...]
    if both.shape[0] > 2 * CHUNK:
        square = jnp.zeros((8, LANES), F32)
        for t in range(2 * TILES):
            tile = eight(a_ref, t * CASES) + eight(b_ref, t * CASES)
            square = square + tile * tile
        sums = both[2 * CHUNK :] + placed_sums([(3, square)])
        both = jnp.concatenate([both[: 2 * CHUNK], sums], axis=0)
    for z in range(out_ref.shape[0]):
        out_ref[z] = both
    held[...] = jnp.where(half == 0, both[:CHUNK], both[CHUNK : 2 * CHUNK])
    backs = []
    for k in range(2):
        tiles = [eight(held, (k * 9 + t) * CASES) for t in range(3)]
        terms = []
        for i, v in enumerate(spread(*tiles)):
            v = jnp.where(rows_live((8, LANES), 1, live_ref[k], i), v, 0.0)
            y = halves(v)
            out = jnp.dot(y[:, :BLOCK], k_ref[k * FACE + i], preferred_element_type=F32)
            terms.append(out[:8] + out[8:])
        backs.append(packed(*terms))
    send_sides(at_ref[1], backs[0], backs[1], near_out, far_out)


def combined(sums_ref, rhs_ref, v_ref, image_ref, w_ref, second_ref, sol_ref, res_ref):
    sums = sums_ref[0]
    for s in range(1, sums_ref.shape[0]):
        sums = sums + sums_ref[s]
    rz, curv, cross, last = (sums[:CASES, n : n + 1] for n in range(4))
    step = rz / curv
    ratio = (step * step * cross - rz) / rz
    grown = 1.0 + ratio
    curv_next = grown * grown * curv - 2.0 * grown * step * cross + step * step * last
    step_next = ratio * rz / curv_next
    on_first = step + step_next * grown
    on_second = step_next * step
    v, w = v_ref[:CASES, :], w_ref[:CASES, :]
    sol = on_first * v - on_second * w
    change = on_second * second_ref[:CASES, :] - on_first * image_ref[:CASES, :]
    for c in range(CASES):
        sol_ref[c] = sol[c : c + 1]
        res_ref[c] = rhs_ref[c] + change[c : c + 1]


SMEM = pl.BlockSpec(memory_space=pltpu.SMEM)
VMEM = pl.BlockSpec(memory_space=pltpu.VMEM)


def shaped(*shape, dtype=F32):
    return jax.ShapeDtypeStruct(shape, dtype)


def in_hbm(value):
    return pltpu.with_memory_space_constraint(value, pltpu.HBM)


def call(kernel, scalars, arrays, out_shape, scratch=(), stays=0, limit=20):
    held = len(arrays) - stays
    return pl.pallas_call(
        kernel,
        in_specs=[SMEM] * len(scalars)
        + [VMEM] * held
        + [pl.BlockSpec(memory_space=pltpu.HBM)] * stays,
        out_specs=tuple(VMEM for _ in out_shape),
        out_shape=tuple(out_shape),
        scratch_shapes=list(scratch),
        compiler_params=pltpu.CompilerParams(vmem_limit_bytes=limit * MIB),
    )(*scalars, *arrays)


def body(rhs, dshift, stiff, face_k, elem_col, elem_row, face_rows):
    span = rhs.shape[2]
    face_len = FACE * BLOCK
    columns, targets = in_hbm(elem_col[0]), in_hbm(elem_row[0])
    live = in_hbm(face_rows[0])
    rhs = in_hbm(rhs.reshape(CASES, 1, span))
    dshift = in_hbm(dshift)
    core = lax.axis_index("slab_2")
    place = jnp.stack([lax.axis_index("dom_1"), core]).astype(jnp.int32)
    z_count = lax.axis_size("dom_0")
    slabs = lax.axis_size(SLAB)
    swap = [(0, 1), (1, 0)]
    across = [(s, (s - 1 if s % 2 == 0 else s + 1) % slabs) for s in range(slabs)]
    face = shaped(8, face_len)
    vector = shaped(8, span)

    def exchanged(near, far):
        return lax.ppermute(near, "slab_2", swap), lax.ppermute(far, SLAB, across)

    faces, face_sq = call(
        face_prep,
        [live],
        [in_hbm(face_k[0])],
        [shaped(2 * FACE, BLOCK, LANES, dtype=BF16), shaped(2, 8, face_len)],
        [pltpu.VMEM((CHUNK * 8, LANES), F32)],
    )
    sq_near, sq_far = exchanged(
        jnp.where(core == 0, face_sq[1], face_sq[0]), jnp.where(core == 0, face_sq[0], face_sq[1])
    )

    blocks, inner = pl.pallas_call(
        stiff_prep,
        grid_spec=pltpu.PrefetchScalarGridSpec(
            num_scalar_prefetch=1,
            grid=(STEPS,),
            in_specs=[pl.BlockSpec((GROUP, BLOCK * BLOCK), lambda i, *_: (i, 0))],
            out_specs=(
                pl.BlockSpec((GROUP, BLOCK, LANES), lambda i, *_: (i, 0, 0)),
                pl.BlockSpec((8, span), lambda i, *_: (0, 0)),
            ),
            scratch_shapes=[
                pltpu.VMEM((CHUNK * 16, LANES), F32),
                pltpu.VMEM((OWN, 8, LANES), F32),
            ],
        ),
        out_shape=(pltpu.HBM((STORED, BLOCK, LANES), BF16), vector),
        compiler_params=pltpu.CompilerParams(vmem_limit_bytes=16 * MIB),
    )(columns, in_hbm(stiff[0]))
    blocks = in_hbm(blocks)

    held = pltpu.VMEM((8, span), F32)
    cols = pltpu.VMEM((OWN, 16, LANES), BF16)
    rows = pltpu.VMEM((SLAB_ROWS, 16, LANES), BF16)
    acc = pltpu.VMEM((SLAB_ROWS, 8, LANES), F32)
    stored = [pltpu.VMEM((STORED, BLOCK, LANES), BF16), pltpu.SemaphoreType.DMA((STEPS,))]

    def all_rows(parts, near, far, sums=()):
        near, far = exchanged(near, far)
        parts = parts.reshape(z_count, 2 * CHUNK, LANES)
        arrived = lax.all_to_all(parts, "dom_0", 0, 0, tiled=True)
        depth = 2 * CHUNK + 8 * len(sums)
        (mine,) = call(
            summed,
            [place, live],
            [arrived, near, far, faces, *sums],
            [shaped(depth, LANES)],
        )
        other = lax.ppermute(mine, "dom_1", swap)
        copies, near, far = call(
            finished,
            [place, live],
            [mine, other, faces],
            [shaped(z_count, depth, LANES), face, face],
            [pltpu.VMEM((CHUNK, LANES), F32)],
        )
        full = lax.all_to_all(copies, "dom_0", 0, 0, tiled=True)
        near, far = exchanged(near, far)
        return full, near, far

    parts, inverse, first, near, far = call(
        first_product,
        [columns, targets, place],
        [rhs, dshift, inner, sq_near, sq_far, blocks],
        [shaped(OWN * CHUNK, LANES), vector, vector, face, face],
        [held, cols, acc, *stored],
        stays=1,
    )
    full, near, far = all_rows(parts, near, far)
    parts, image, second, sums, near, far = call(
        middle_product,
        [columns, targets, place],
        [full.reshape(-1, LANES), rhs, dshift, inverse, first, near, far, blocks],
        [shaped(OWN * CHUNK, LANES), vector, vector, shaped(8, LANES), face, face],
        [held, rows, cols, acc, *stored],
        stays=1,
    )
    full, near, far = all_rows(parts, near, far, [sums])
    full, near, far = lax.optimization_barrier((full, near, far))
    sums = jnp.sum(full[:, 2 * CHUNK :], axis=0)
    sums = lax.all_to_all(
        jnp.broadcast_to(sums[None], (slabs, *sums.shape)), SLAB, 0, 0, tiled=True
    )
    (second_image,) = call(
        last_product,
        [columns, targets, place],
        [full.reshape(-1, LANES), dshift, second, near, far, blocks],
        [vector],
        [rows, pltpu.VMEM((OWN, 8, LANES), F32), *stored],
        stays=1,
    )
    out = shaped(CASES, 1, span)
    return call(combined, [], [sums, rhs, first, image, second, second_image], [out, out])


def solution(mesh):
    finer = Mesh(
        mesh.devices.reshape(4, 2, 2, 8, 2), ("slab_0", "slab_1", "slab_2", "dom_0", "dom_1")
    )
    placed = (
        P(None, SLAB, DOM),
        P(SLAB, DOM),
        P(SLAB, DOM, None),
        P(SLAB, None, DOM, None),
        P(SLAB, DOM),
        P(SLAB, DOM),
        P(SLAB, None),
    )
    return jax.shard_map(
        body,
        mesh=finer,
        in_specs=placed,
        out_specs=(P(None, SLAB, DOM), P(None, SLAB, DOM)),
        check_vma=False,
    )
```

```python
import functools

import jax
import jax.numpy as jnp
from jax import lax
from jax.experimental import pallas as pl
from jax.experimental.pallas import tpu as pltpu
from jax.sharding import Mesh
from jax.sharding import PartitionSpec as P

BLOCK = 96
CASES = 6
DOM = ("dom_0", "dom_1")
SLAB = ("slab_0", "slab_1", "slab_2")
F32 = jnp.float32
BF16 = jnp.bfloat16
LANES = 128
OWN = 16
STORED = 256
SLAB_ROWS = 256
GROUP = 32
STEPS = STORED // GROUP
CHUNK = 72
TILES = 12
FACE = 4
MIB = 1024 * 1024


def lane(rows):
    return lax.broadcasted_iota(jnp.int32, (rows, LANES), 1)


def spread(t0, t1, t2):
    at = lane(t0.shape[0])
    v0 = t0
    v1 = jnp.where(at < 32, pltpu.roll(t0, 32, 1), pltpu.roll(t1, 32, 1))
    v2 = jnp.where(at < 64, pltpu.roll(t1, 64, 1), pltpu.roll(t2, 64, 1))
    v3 = pltpu.roll(t2, 96, 1)
    return [jnp.where(at < BLOCK, v, 0.0) for v in (v0, v1, v2, v3)]


def packed(v0, v1, v2, v3):
    at = lane(v0.shape[0])
    r1 = pltpu.roll(v1, 96, 1)
    r2 = pltpu.roll(v2, 64, 1)
    r3 = pltpu.roll(v3, 32, 1)
    return (
        jnp.where(at < 96, v0, r1),
        jnp.where(at < 64, r1, r2),
        jnp.where(at < 32, r2, r3),
    )


def halves(v):
    high = v.astype(BF16).astype(F32)
    return jnp.concatenate([high, v - high], axis=0).astype(BF16)


def rows_live(shape, dim, live, block):
    at = lax.broadcasted_iota(jnp.int32, shape, dim)
    row = 4 * (at % 24) + at // 24
    return row + block * BLOCK < live


def eight(ref, start):
    if start + 8 <= ref.shape[0]:
        return ref[start : start + 8, :]
    return pltpu.roll(ref[start - 2 : start + 6, :], 6, 0)


def block_of(held, first, stride):
    parts = [held[pl.ds(first + k * (stride // 3), 24, stride=stride), :] for k in range(3)]
    return jnp.concatenate(spread(*parts), axis=0)


def face_prep(live_ref, x_ref, k_ref, sq_ref, held):
    for k in range(2):
        for t in range(CHUNK):
            held[t * 8 + k * FACE : t * 8 + (k + 1) * FACE, :] = x_ref[
                k, :, t * LANES : (t + 1) * LANES
            ].astype(F32)
    for k in range(2):
        sums = []
        for i in range(FACE):
            whole = block_of(held, k * FACE + i, 24)
            k_ref[k * FACE + i] = whole.astype(BF16)
            masked = jnp.where(rows_live((BLOCK, LANES), 0, live_ref[k], i), whole, 0.0)
            total = jnp.sum(masked * masked, axis=0, keepdims=True)
            sums.append(jnp.broadcast_to(total, (8, LANES)))
        for t, tile in enumerate(packed(*sums)):
            sq_ref[k, :, t * LANES : (t + 1) * LANES] = tile


def stiff_prep(col_ref, x_ref, k_ref, diag_ref, held, acc):
    step = pl.program_id(0)

    @pl.when(step == 0)
    def _():
        acc[...] = jnp.zeros_like(acc)

    for half in range(GROUP // 16):
        for t in range(CHUNK):
            held[t * 16 : (t + 1) * 16, :] = x_ref[
                half * 16 : (half + 1) * 16, t * LANES : (t + 1) * LANES
            ].astype(F32)
        for e in range(16):
            whole = block_of(held, e, 48)
            k_ref[half * 16 + e] = whole.astype(BF16)
            total = jnp.sum((whole * whole).reshape(12, 8, LANES), axis=0)
            j = col_ref[step * GROUP + half * 16 + e]
            acc[j] = acc[j] + total

    @pl.when(step == STEPS - 1)
    def _():
        for q in range(OWN // 4):
            sums = [
                jnp.broadcast_to(jnp.sum(acc[q * 4 + i], axis=0, keepdims=True), (8, LANES))
                for i in range(4)
            ]
            for t, tile in enumerate(packed(*sums)):
                diag_ref[:, tile_at(q * 3 + t)] = tile


def tile_at(t):
    return slice(t * LANES, (t + 1) * LANES)


def part(g):
    return pl.ds(g * GROUP, GROUP)


def fetch(k_any, k_ref, sems):
    for g in range(STEPS):
        pltpu.make_async_copy(k_any.at[part(g)], k_ref.at[part(g)], sems.at[g]).start()


def fetched(k_any, k_ref, sems, g):
    pltpu.make_async_copy(k_any.at[part(g)], k_ref.at[part(g)], sems.at[g]).wait()


def forward(col_ref, row_ref, tiles, k_ref, out_ref, cols, acc, wait=None):
    for q in range(OWN // 4):
        for i, v in enumerate(spread(*tiles[q * 3 : q * 3 + 3])):
            cols[q * 4 + i] = halves(v)
    acc[...] = jnp.zeros_like(acc)

    def group(g, carry):
        base = g * GROUP
        if wait is not None:
            wait(g)
        for first in range(0, GROUP, 8):
            terms = []
            for e in range(first, first + 8):
                x = cols[col_ref[base + e]]
                out = lax.dot_general(
                    x, k_ref[base + e], (((1,), (1,)), ((), ())), preferred_element_type=F32
                )
                terms.append(out[:8] + out[8:])
            for e in range(first, first + 8):
                r = row_ref[base + e]
                acc[r, :, :BLOCK] = acc[r, :, :BLOCK] + terms[e - first]
        return carry

    lax.fori_loop(0, STEPS, group, 0)
    for g in range(SLAB_ROWS // 4):
        for t, tile in enumerate(packed(*[acc[g * 4 + i] for i in range(4)])):
            at = (g // 4) * CHUNK + ((g % 4) * 3 + t) * CASES
            out_ref[at : at + CASES, :] = tile[:CASES]


def adjoint(col_ref, row_ref, y_ref, k_ref, rows, acc, wait):
    depth = y_ref.shape[0] // (OWN // 2)
    for g in range(SLAB_ROWS // 4):
        at = (g // 8) * depth + (g // 4 % 2) * CHUNK + (g % 4) * 3 * CASES
        tiles = [eight(y_ref, at + t * CASES) for t in range(3)]
        for i, v in enumerate(spread(*tiles)):
            rows[g * 4 + i] = halves(v)
    acc[...] = jnp.zeros_like(acc)

    def group(g, carry):
        base = g * GROUP
        wait(g)
        for first in range(0, GROUP, 8):
            terms = []
            for e in range(first, first + 8):
                y = rows[row_ref[base + e]]
                out = jnp.dot(y[:, :BLOCK], k_ref[base + e], preferred_element_type=F32)
                terms.append(out[:8] + out[8:])
            for e in range(first, first + 8):
                j = col_ref[base + e]
                acc[j] = acc[j] + terms[e - first]
        return carry

    lax.fori_loop(0, STEPS, group, 0)
    tiles = []
    for q in range(OWN // 4):
        tiles += packed(*[acc[q * 4 + i] for i in range(4)])
    return tiles


def both_sides(core, near_ref, far_ref):
    near = [near_ref[:, tile_at(t)] for t in range(3)]
    far = [far_ref[:, tile_at(t)] for t in range(3)]
    below = [jnp.where(core == 0, f, n) for n, f in zip(near, far)]
    above = [jnp.where(core == 0, n, f) for n, f in zip(near, far)]
    return below, above


def send_sides(core, lower, upper, near_ref, far_ref):
    for t in range(3):
        near_ref[:, tile_at(t)] = jnp.where(core == 0, upper[t], lower[t])
        far_ref[:, tile_at(t)] = jnp.where(core == 0, lower[t], upper[t])


def first_vector(
    at_ref, rhs_ref, shift_ref, diag_ref, near_ref, far_ref,
    inverse_ref, v_ref, near_out, far_out, held,
):
    core = at_ref[1]
    held[...] = jnp.zeros_like(held)
    for c in range(CASES):
        held[c : c + 1, :] = rhs_ref[c]
    below, above = both_sides(core, near_ref, far_ref)
    tiles = []
    for t in range(TILES):
        total = diag_ref[:, tile_at(t)] + shift_ref[:, tile_at(t)]
        if t < 3:
            total = total + below[t]
        if t >= 9:
            total = total + above[t - 9]
        inverse = 1.0 / total
        inverse_ref[:, tile_at(t)] = inverse
        tile = inverse * held[:, tile_at(t)]
        v_ref[:, tile_at(t)] = tile
        tiles.append(tile)
    send_sides(core, tiles[:3], tiles[9:], near_out, far_out)


def forward_product(col_ref, row_ref, v_ref, k_any, out_ref, cols, acc, k_ref, sems):
    fetch(k_any, k_ref, sems)
    wait = functools.partial(fetched, k_any, k_ref, sems)
    tiles = [v_ref[:, tile_at(t)] for t in range(TILES)]
    forward(col_ref, row_ref, tiles, k_ref, out_ref, cols, acc, wait)


def adjoint_product(col_ref, row_ref, y_ref, k_any, out_ref, rows, acc, k_ref, sems):
    fetch(k_any, k_ref, sems)
    wait = functools.partial(fetched, k_any, k_ref, sems)
    for t, tile in enumerate(adjoint(col_ref, row_ref, y_ref, k_ref, rows, acc, wait)):
        out_ref[:, tile_at(t)] = tile


def image_tiles(core, part_ref, v_ref, shift_ref, near_ref, far_ref):
    below, above = both_sides(core, near_ref, far_ref)
    whole = [
        part_ref[:, tile_at(t)] + shift_ref[:, tile_at(t)] * v_ref[:, tile_at(t)]
        for t in range(TILES)
    ]
    return (
        [whole[t] + below[t] for t in range(3)]
        + whole[3:9]
        + [whole[t + 9] + above[t] for t in range(3)]
    )


def placed_sums(values):
    at = lane(8)
    out = jnp.zeros((8, LANES), F32)
    for n, value in values:
        out = jnp.where(at == n, jnp.sum(value, axis=1, keepdims=True), out)
    return out


def second_vector(
    at_ref, part_ref, rhs_ref, shift_ref, inverse_ref, v_ref, near_ref, far_ref,
    image_ref, w_ref, sums_ref, near_out, far_out, held,
):
    core = at_ref[1]
    held[...] = jnp.zeros_like(held)
    for c in range(CASES):
        held[c : c + 1, :] = rhs_ref[c]
    sums = [jnp.zeros((8, LANES), F32) for _ in range(4)]
    second = []
    tiles = image_tiles(core, part_ref, v_ref, shift_ref, near_ref, far_ref)
    for t, image in enumerate(tiles):
        image_ref[:, tile_at(t)] = image
        w = inverse_ref[:, tile_at(t)] * image
        w_ref[:, tile_at(t)] = w
        second.append(w)
        v = v_ref[:, tile_at(t)]
        sums[0] = sums[0] + held[:, tile_at(t)] * v
        sums[1] = sums[1] + v * image
        sums[2] = sums[2] + image * w
        sums[3] = sums[3] + shift_ref[:, tile_at(t)] * w * w
    sums_ref[...] = placed_sums(enumerate(sums))
    send_sides(core, second[:3], second[9:], near_out, far_out)


def summed(at_ref, live_ref, y_ref, near_ref, far_ref, k_ref, *rest):
    out_ref = rest[-1]
    half = at_ref[0]
    whole = y_ref[0]
    for z in range(1, y_ref.shape[0]):
        whole = whole + y_ref[z]
    out_ref[: 2 * CHUNK, :] = whole
    if len(rest) > 1:
        out_ref[2 * CHUNK :, :] = rest[0][...]
    for k, face in enumerate(both_sides(at_ref[1], near_ref, far_ref)):
        terms = []
        for i, v in enumerate(spread(*face)):
            out = lax.dot_general(
                halves(v), k_ref[k * FACE + i], (((1,), (1,)), ((), ())), preferred_element_type=F32
            )
            term = out[:8] + out[8:]
            term = jnp.where(rows_live((8, BLOCK), 1, live_ref[k], i), term, 0.0)
            terms.append(jnp.concatenate([term, jnp.zeros((8, LANES - BLOCK), F32)], axis=1))
        for t, tile in enumerate(packed(*terms)):
            for h in range(2):
                at = h * CHUNK + (k * 9 + t) * CASES
                added = jnp.where(half == h, tile[:CASES], 0.0)
                out_ref[at : at + CASES, :] = out_ref[at : at + CASES, :] + added


def finished(at_ref, live_ref, a_ref, b_ref, k_ref, out_ref, near_out, far_out, held):
    half = at_ref[0]
    both = a_ref[...] + b_ref[...]
    if both.shape[0] > 2 * CHUNK:
        square = jnp.zeros((8, LANES), F32)
        for t in range(2 * TILES):
            tile = eight(a_ref, t * CASES) + eight(b_ref, t * CASES)
            square = square + tile * tile
        sums = both[2 * CHUNK :] + placed_sums([(3, square)])
        both = jnp.concatenate([both[: 2 * CHUNK], sums], axis=0)
    for z in range(out_ref.shape[0]):
        out_ref[z] = both
    held[...] = jnp.where(half == 0, both[:CHUNK], both[CHUNK : 2 * CHUNK])
    backs = []
    for k in range(2):
        tiles = [eight(held, (k * 9 + t) * CASES) for t in range(3)]
        terms = []
        for i, v in enumerate(spread(*tiles)):
            v = jnp.where(rows_live((8, LANES), 1, live_ref[k], i), v, 0.0)
            y = halves(v)
            out = jnp.dot(y[:, :BLOCK], k_ref[k * FACE + i], preferred_element_type=F32)
            terms.append(out[:8] + out[8:])
        backs.append(packed(*terms))
    send_sides(at_ref[1], backs[0], backs[1], near_out, far_out)


def combined(
    at_ref, sums_ref, rhs_ref, shift_ref, v_ref, image_ref, w_ref, part_ref, near_ref, far_ref,
    sol_ref, res_ref,
):
    sums = sums_ref[0]
    for s in range(1, sums_ref.shape[0]):
        sums = sums + sums_ref[s]
    rz, curv, cross, last = (sums[:, n : n + 1] for n in range(4))
    step = rz / curv
    ratio = (step * step * cross - rz) / rz
    grown = 1.0 + ratio
    curv_next = grown * grown * curv - 2.0 * grown * step * cross + step * step * last
    step_next = ratio * rz / curv_next
    on_first = step + step_next * grown
    on_second = step_next * step
    tiles = image_tiles(at_ref[1], part_ref, w_ref, shift_ref, near_ref, far_ref)
    for t, second in enumerate(tiles):
        to = tile_at(t)
        sol = on_first * v_ref[:, to] - on_second * w_ref[:, to]
        change = on_second * second - on_first * image_ref[:, to]
        for c in range(CASES):
            sol_ref[c, :, to] = sol[c : c + 1]
            res_ref[c, :, to] = rhs_ref[c, :, to] + change[c : c + 1]


SMEM = pl.BlockSpec(memory_space=pltpu.SMEM)
VMEM = pl.BlockSpec(memory_space=pltpu.VMEM)


def shaped(*shape, dtype=F32):
    return jax.ShapeDtypeStruct(shape, dtype)


def in_hbm(value):
    return pltpu.with_memory_space_constraint(value, pltpu.HBM)


def call(kernel, scalars, arrays, out_shape, scratch=(), stays=0, limit=20):
    held = len(arrays) - stays
    return pl.pallas_call(
        kernel,
        in_specs=[SMEM] * len(scalars)
        + [VMEM] * held
        + [pl.BlockSpec(memory_space=pltpu.HBM)] * stays,
        out_specs=tuple(VMEM for _ in out_shape),
        out_shape=tuple(out_shape),
        scratch_shapes=list(scratch),
        compiler_params=pltpu.CompilerParams(vmem_limit_bytes=limit * MIB),
    )(*scalars, *arrays)


def body(rhs, dshift, stiff, face_k, elem_col, elem_row, face_rows):
    span = rhs.shape[2]
    face_len = FACE * BLOCK
    columns, targets = in_hbm(elem_col[0]), in_hbm(elem_row[0])
    live = in_hbm(face_rows[0])
    rhs = in_hbm(rhs.reshape(CASES, 1, span))
    dshift = in_hbm(dshift)
    core = lax.axis_index("slab_2")
    place = jnp.stack([lax.axis_index("dom_1"), core]).astype(jnp.int32)
    z_count = lax.axis_size("dom_0")
    slabs = lax.axis_size(SLAB)
    swap = [(0, 1), (1, 0)]
    across = [(s, (s - 1 if s % 2 == 0 else s + 1) % slabs) for s in range(slabs)]
    face = shaped(8, face_len)
    vector = shaped(8, span)

    def exchanged(near, far):
        return lax.ppermute(near, "slab_2", swap), lax.ppermute(far, SLAB, across)

    faces, face_sq = call(
        face_prep,
        [live],
        [in_hbm(face_k[0])],
        [shaped(2 * FACE, BLOCK, LANES, dtype=BF16), shaped(2, 8, face_len)],
        [pltpu.VMEM((CHUNK * 8, LANES), F32)],
    )
    sq_near, sq_far = exchanged(
        jnp.where(core == 0, face_sq[1], face_sq[0]), jnp.where(core == 0, face_sq[0], face_sq[1])
    )

    blocks, inner = pl.pallas_call(
        stiff_prep,
        grid_spec=pltpu.PrefetchScalarGridSpec(
            num_scalar_prefetch=1,
            grid=(STEPS,),
            in_specs=[pl.BlockSpec((GROUP, BLOCK * BLOCK), lambda i, *_: (i, 0))],
            out_specs=(
                pl.BlockSpec((GROUP, BLOCK, LANES), lambda i, *_: (i, 0, 0)),
                pl.BlockSpec((8, span), lambda i, *_: (0, 0)),
            ),
            scratch_shapes=[
                pltpu.VMEM((CHUNK * 16, LANES), F32),
                pltpu.VMEM((OWN, 8, LANES), F32),
            ],
        ),
        out_shape=(pltpu.HBM((STORED, BLOCK, LANES), BF16), vector),
        compiler_params=pltpu.CompilerParams(vmem_limit_bytes=16 * MIB),
    )(columns, in_hbm(stiff[0]))
    blocks = in_hbm(blocks)

    held = pltpu.VMEM((8, span), F32)
    cols = pltpu.VMEM((OWN, 16, LANES), BF16)
    rows = pltpu.VMEM((SLAB_ROWS, 16, LANES), BF16)
    acc = pltpu.VMEM((SLAB_ROWS, 8, LANES), F32)
    stored = [pltpu.VMEM((STORED, BLOCK, LANES), BF16), pltpu.SemaphoreType.DMA((STEPS,))]

    def all_rows(vector, near, far, sums=()):
        near, far = exchanged(near, far)
        (parts,) = call(
            forward_product,
            [columns, targets],
            [vector, blocks],
            [shaped(OWN * CHUNK, LANES)],
            [cols, acc, *stored],
            stays=1,
        )
        parts = parts.reshape(z_count, 2 * CHUNK, LANES)
        parts, near, far = lax.optimization_barrier((parts, near, far))
        arrived = lax.all_to_all(parts, "dom_0", 0, 0, tiled=True)
        depth = 2 * CHUNK + 8 * len(sums)
        (mine,) = call(
            summed,
            [place, live],
            [arrived, near, far, faces, *sums],
            [shaped(depth, LANES)],
        )
        other = lax.ppermute(mine, "dom_1", swap)
        copies, near, far = call(
            finished,
            [place, live],
            [mine, other, faces],
            [shaped(z_count, depth, LANES), face, face],
            [pltpu.VMEM((CHUNK, LANES), F32)],
        )
        full = lax.all_to_all(copies, "dom_0", 0, 0, tiled=True)
        full, near, far = lax.optimization_barrier((full, near, far))
        near, far = exchanged(near, far)
        return full, near, far

    def adjoint_part(full):
        return call(
            adjoint_product,
            [columns, targets],
            [full.reshape(-1, LANES), blocks],
            [vector],
            [rows, pltpu.VMEM((OWN, 8, LANES), F32), *stored],
            stays=1,
        )[0]

    inverse, first, near, far = call(
        first_vector,
        [place],
        [rhs, dshift, inner, sq_near, sq_far],
        [vector, vector, face, face],
        [held],
    )
    full, near, far = all_rows(first, near, far)
    part_of = adjoint_part(full)
    image, second, sums, near, far = call(
        second_vector,
        [place],
        [part_of, rhs, dshift, inverse, first, near, far],
        [vector, vector, shaped(8, LANES), face, face],
        [held],
    )
    full, near, far = all_rows(second, near, far, [sums])
    sums = jnp.sum(full[:, 2 * CHUNK :], axis=0)
    sums = lax.all_to_all(
        jnp.broadcast_to(sums[None], (slabs, *sums.shape)), SLAB, 0, 0, tiled=True
    )
    out = shaped(CASES, 1, span)
    return call(
        combined,
        [place],
        [sums, rhs, dshift, first, image, second, adjoint_part(full), near, far],
        [out, out],
    )


def solution(mesh):
    finer = Mesh(
        mesh.devices.reshape(4, 2, 2, 8, 2), ("slab_0", "slab_1", "slab_2", "dom_0", "dom_1")
    )
    placed = (
        P(None, SLAB, DOM),
        P(SLAB, DOM),
        P(SLAB, DOM, None),
        P(SLAB, None, DOM, None),
        P(SLAB, DOM),
        P(SLAB, DOM),
        P(SLAB, None),
    )
    return jax.shard_map(
        body,
        mesh=finer,
        in_specs=placed,
        out_specs=(P(None, SLAB, DOM), P(None, SLAB, DOM)),
        check_vma=False,
    )
```

```python
import functools

import jax
import jax.numpy as jnp
from jax import lax
from jax.experimental import pallas as pl
from jax.experimental.pallas import tpu as pltpu
from jax.sharding import Mesh
from jax.sharding import PartitionSpec as P

BLOCK = 96
CASES = 6
DOM = ("dom_0", "dom_1")
SLAB = ("slab_0", "slab_1", "slab_2")
F32 = jnp.float32
BF16 = jnp.bfloat16
LANES = 128
OWN = 16
STORED = 256
SLAB_ROWS = 256
GROUP = 32
STEPS = STORED // GROUP
CHUNK = 72
TILES = 12
FACE = 4
MIB = 1024 * 1024


def lane(rows):
    return lax.broadcasted_iota(jnp.int32, (rows, LANES), 1)


def spread(t0, t1, t2):
    at = lane(t0.shape[0])
    v0 = t0
    v1 = jnp.where(at < 32, pltpu.roll(t0, 32, 1), pltpu.roll(t1, 32, 1))
    v2 = jnp.where(at < 64, pltpu.roll(t1, 64, 1), pltpu.roll(t2, 64, 1))
    v3 = pltpu.roll(t2, 96, 1)
    return [jnp.where(at < BLOCK, v, 0.0) for v in (v0, v1, v2, v3)]


def packed(v0, v1, v2, v3):
    at = lane(v0.shape[0])
    r1 = pltpu.roll(v1, 96, 1)
    r2 = pltpu.roll(v2, 64, 1)
    r3 = pltpu.roll(v3, 32, 1)
    return (
        jnp.where(at < 96, v0, r1),
        jnp.where(at < 64, r1, r2),
        jnp.where(at < 32, r2, r3),
    )


def halves(v):
    high = v.astype(BF16).astype(F32)
    return jnp.concatenate([high, v - high], axis=0).astype(BF16)


def rows_live(shape, dim, live, block):
    at = lax.broadcasted_iota(jnp.int32, shape, dim)
    row = 4 * (at % 24) + at // 24
    return row + block * BLOCK < live


def eight(ref, start):
    if start + 8 <= ref.shape[0]:
        return ref[start : start + 8, :]
    return pltpu.roll(ref[start - 2 : start + 6, :], 6, 0)


def block_of(held, first, stride):
    parts = [held[pl.ds(first + k * (stride // 3), 24, stride=stride), :] for k in range(3)]
    return jnp.concatenate(spread(*parts), axis=0)


def face_prep(live_ref, x_ref, k_ref, sq_ref, held):
    for k in range(2):
        for t in range(CHUNK):
            held[t * 8 + k * FACE : t * 8 + (k + 1) * FACE, :] = x_ref[
                k, :, t * LANES : (t + 1) * LANES
            ].astype(F32)
    for k in range(2):
        sums = []
        for i in range(FACE):
            whole = block_of(held, k * FACE + i, 24)
            k_ref[k * FACE + i] = whole.astype(BF16)
            masked = jnp.where(rows_live((BLOCK, LANES), 0, live_ref[k], i), whole, 0.0)
            total = jnp.sum(masked * masked, axis=0, keepdims=True)
            sums.append(jnp.broadcast_to(total, (8, LANES)))
        for t, tile in enumerate(packed(*sums)):
            sq_ref[k, :, t * LANES : (t + 1) * LANES] = tile


def stiff_prep(col_ref, x_any, k_any, diag_ref, x_ref, k_ref, held, acc, came, left):
    def arriving(g):
        return pltpu.make_async_copy(x_any.at[part(g)], x_ref.at[part(g)], came.at[g])

    def leaving(g):
        return pltpu.make_async_copy(k_ref.at[part(g)], k_any.at[part(g)], left.at[g])

    for g in range(STEPS):
        arriving(g).start()
    acc[...] = jnp.zeros_like(acc)

    def group(g, carry):
        arriving(g).wait()
        for half in range(GROUP // 16):
            base = g * GROUP + half * 16
            for t in range(CHUNK):
                held[t * 16 : (t + 1) * 16, :] = x_ref[
                    pl.ds(pl.multiple_of(base, 16), 16), tile_at(t)
                ].astype(F32)
            for e in range(16):
                whole = block_of(held, e, 48)
                k_ref[base + e] = whole.astype(BF16)
                total = jnp.sum((whole * whole).reshape(12, 8, LANES), axis=0)
                j = col_ref[base + e]
                acc[j] = acc[j] + total
        leaving(g).start()
        return carry

    lax.fori_loop(0, STEPS, group, 0)
    for q in range(OWN // 4):
        sums = [
            jnp.broadcast_to(jnp.sum(acc[q * 4 + i], axis=0, keepdims=True), (8, LANES))
            for i in range(4)
        ]
        for t, tile in enumerate(packed(*sums)):
            diag_ref[:, tile_at(q * 3 + t)] = tile
    for g in range(STEPS):
        leaving(g).wait()


def tile_at(t):
    return slice(t * LANES, (t + 1) * LANES)


def part(g):
    return pl.ds(g * GROUP, GROUP)


def brought(k_any, k_ref, sems, g):
    return pltpu.make_async_copy(k_any.at[part(g)], k_ref.at[part(g), pl.ds(0, BLOCK)], sems.at[g])


def fetch(k_any, k_ref, sems):
    for g in range(STEPS):
        brought(k_any, k_ref, sems, g).start()


def fetched(k_any, k_ref, sems, g):
    brought(k_any, k_ref, sems, g).wait()


def forward(col_ref, row_ref, tiles, k_ref, out_ref, cols, acc, wait=None):
    for q in range(OWN // 4):
        for i, v in enumerate(spread(*tiles[q * 3 : q * 3 + 3])):
            cols[q * 4 + i] = halves(v)
    acc[...] = jnp.zeros_like(acc)

    def group(g, carry):
        base = g * GROUP
        if wait is not None:
            wait(g)
        for first in range(0, GROUP, 8):
            terms = []
            for e in range(first, first + 8, 2):
                x = jnp.concatenate([cols[col_ref[base + e]], cols[col_ref[base + e + 1]]], axis=0)
                two = k_ref[pl.ds(base + e, 2)].reshape(2 * LANES, LANES)
                out = lax.dot_general(
                    x, two, (((1,), (1,)), ((), ())), preferred_element_type=F32
                )
                terms.append(out[:8, :BLOCK] + out[8:16, :BLOCK])
                other = slice(LANES, LANES + BLOCK)
                terms.append(out[16:24, other] + out[24:, other])
            for e in range(first, first + 8):
                r = row_ref[base + e]
                acc[r, :, :BLOCK] = acc[r, :, :BLOCK] + terms[e - first]
        return carry

    lax.fori_loop(0, STEPS, group, 0)
    for g in range(SLAB_ROWS // 4):
        for t, tile in enumerate(packed(*[acc[g * 4 + i] for i in range(4)])):
            at = (g // 4) * CHUNK + ((g % 4) * 3 + t) * CASES
            out_ref[at : at + CASES, :] = tile[:CASES]


def adjoint(col_ref, row_ref, y_ref, k_ref, rows, acc, wait):
    depth = y_ref.shape[0] // (SLAB_ROWS // OWN)
    for g in range(SLAB_ROWS // 4):
        at = (g // 4) * depth + (g % 4) * 3 * CASES
        tiles = [eight(y_ref, at + t * CASES) for t in range(3)]
        for i, v in enumerate(spread(*tiles)):
            rows[g * 4 + i] = halves(v)
    acc[...] = jnp.zeros_like(acc)

    def group(g, carry):
        base = g * GROUP
        wait(g)
        for first in range(0, GROUP, 8):
            terms = []
            for e in range(first, first + 8, 2):
                y = jnp.concatenate([rows[row_ref[base + e]], rows[row_ref[base + e + 1]]], axis=0)
                two = jnp.concatenate([k_ref[base + e, :BLOCK], k_ref[base + e + 1, :BLOCK]], axis=1)
                out = jnp.dot(y[:, :BLOCK], two, preferred_element_type=F32)
                terms.append(out[:8, :LANES] + out[8:16, :LANES])
                terms.append(out[16:24, LANES:] + out[24:, LANES:])
            for e in range(first, first + 8):
                j = col_ref[base + e]
                acc[j] = acc[j] + terms[e - first]
        return carry

    lax.fori_loop(0, STEPS, group, 0)
    tiles = []
    for q in range(OWN // 4):
        tiles += packed(*[acc[q * 4 + i] for i in range(4)])
    return tiles


def both_sides(core, near_ref, far_ref):
    near = [near_ref[:, tile_at(t)] for t in range(3)]
    far = [far_ref[:, tile_at(t)] for t in range(3)]
    below = [jnp.where(core == 0, f, n) for n, f in zip(near, far)]
    above = [jnp.where(core == 0, n, f) for n, f in zip(near, far)]
    return below, above


def send_sides(core, lower, upper, near_ref, far_ref):
    for t in range(3):
        near_ref[:, tile_at(t)] = jnp.where(core == 0, upper[t], lower[t])
        far_ref[:, tile_at(t)] = jnp.where(core == 0, lower[t], upper[t])


def first_product(
    col_ref, row_ref, at_ref, rhs_ref, shift_ref, diag_ref, near_ref, far_ref, k_any,
    out_ref, inverse_ref, v_ref, near_out, far_out, held, cols, acc, k_ref, sems,
):
    fetch(k_any, k_ref, sems)
    core = at_ref[0]
    held[...] = jnp.zeros_like(held)
    for c in range(CASES):
        held[c : c + 1, :] = rhs_ref[c]
    below, above = both_sides(core, near_ref, far_ref)
    tiles = []
    for t in range(TILES):
        total = diag_ref[:, tile_at(t)] + shift_ref[:, tile_at(t)]
        if t < 3:
            total = total + below[t]
        if t >= 9:
            total = total + above[t - 9]
        inverse = 1.0 / total
        inverse_ref[:, tile_at(t)] = inverse
        tile = inverse * held[:, tile_at(t)]
        v_ref[:, tile_at(t)] = tile
        tiles.append(tile)
    send_sides(core, tiles[:3], tiles[9:], near_out, far_out)
    wait = functools.partial(fetched, k_any, k_ref, sems)
    forward(col_ref, row_ref, tiles, k_ref, out_ref, cols, acc, wait)


def image_tiles(core, tiles, v_ref, shift_ref, near_ref, far_ref):
    below, above = both_sides(core, near_ref, far_ref)
    whole = [
        tile + shift_ref[:, tile_at(t)] * v_ref[:, tile_at(t)] for t, tile in enumerate(tiles)
    ]
    return (
        [whole[t] + below[t] for t in range(3)]
        + whole[3:9]
        + [whole[t + 9] + above[t] for t in range(3)]
    )


def placed_sums(values):
    at = lane(8)
    out = jnp.zeros((8, LANES), F32)
    for n, value in values:
        out = jnp.where(at == n, jnp.sum(value, axis=1, keepdims=True), out)
    return out


def middle_product(
    col_ref, row_ref, at_ref, y_ref, rhs_ref, shift_ref, inverse_ref, v_ref, near_ref, far_ref,
    k_any, out_ref, image_ref, w_ref, sums_ref, near_out, far_out, held, rows, cols, acc,
    k_ref, sems,
):
    fetch(k_any, k_ref, sems)
    core = at_ref[0]
    wait = functools.partial(fetched, k_any, k_ref, sems)
    tiles = adjoint(col_ref, row_ref, y_ref, k_ref, rows, acc, wait)
    tiles = image_tiles(core, tiles, v_ref, shift_ref, near_ref, far_ref)
    held[...] = jnp.zeros_like(held)
    for c in range(CASES):
        held[c : c + 1, :] = rhs_ref[c]
    sums = [jnp.zeros((8, LANES), F32) for _ in range(4)]
    second = []
    for t, image in enumerate(tiles):
        image_ref[:, tile_at(t)] = image
        w = inverse_ref[:, tile_at(t)] * image
        w_ref[:, tile_at(t)] = w
        second.append(w)
        v = v_ref[:, tile_at(t)]
        sums[0] = sums[0] + held[:, tile_at(t)] * v
        sums[1] = sums[1] + v * image
        sums[2] = sums[2] + image * w
        sums[3] = sums[3] + shift_ref[:, tile_at(t)] * w * w
    sums_ref[...] = placed_sums(enumerate(sums))
    send_sides(core, second[:3], second[9:], near_out, far_out)
    forward(col_ref, row_ref, second, k_ref, out_ref, cols, acc)


def last_product(
    col_ref, row_ref, at_ref, y_ref, shift_ref, v_ref, near_ref, far_ref, k_any,
    image_ref, rows, acc, k_ref, sems,
):
    fetch(k_any, k_ref, sems)
    wait = functools.partial(fetched, k_any, k_ref, sems)
    tiles = adjoint(col_ref, row_ref, y_ref, k_ref, rows, acc, wait)
    for t, tile in enumerate(image_tiles(at_ref[0], tiles, v_ref, shift_ref, near_ref, far_ref)):
        image_ref[:, tile_at(t)] = tile


def settled(at_ref, live_ref, y_ref, near_ref, far_ref, k_ref, *rest):
    out_ref, near_out, far_out, held = rest[-4:]
    whole = y_ref[0]
    for d in range(1, y_ref.shape[0]):
        whole = whole + y_ref[d]
    held[...] = whole
    for k, face in enumerate(both_sides(at_ref[0], near_ref, far_ref)):
        terms = []
        for i, v in enumerate(spread(*face)):
            out = lax.dot_general(
                halves(v), k_ref[k * FACE + i], (((1,), (1,)), ((), ())), preferred_element_type=F32
            )
            term = out[:8] + out[8:]
            term = jnp.where(rows_live((8, BLOCK), 1, live_ref[k], i), term, 0.0)
            terms.append(jnp.concatenate([term, jnp.zeros((8, LANES - BLOCK), F32)], axis=1))
        for t, tile in enumerate(packed(*terms)):
            at = (k * 9 + t) * CASES
            held[at : at + CASES, :] = held[at : at + CASES, :] + tile[:CASES]
    own = held[...]
    for d in range(out_ref.shape[0]):
        out_ref[d, :CHUNK] = own
    if len(rest) > 4:
        square = jnp.zeros((8, LANES), F32)
        for t in range(TILES):
            tile = eight(held, t * CASES)
            square = square + tile * tile
        sums = rest[0][...] + placed_sums([(3, square)])
        for d in range(out_ref.shape[0]):
            out_ref[d, CHUNK:] = sums
    backs = []
    for k in range(2):
        tiles = [eight(held, (k * 9 + t) * CASES) for t in range(3)]
        terms = []
        for i, v in enumerate(spread(*tiles)):
            v = jnp.where(rows_live((8, LANES), 1, live_ref[k], i), v, 0.0)
            y = halves(v)
            out = jnp.dot(y[:, :BLOCK], k_ref[k * FACE + i], preferred_element_type=F32)
            terms.append(out[:8] + out[8:])
        backs.append(packed(*terms))
    send_sides(at_ref[0], backs[0], backs[1], near_out, far_out)


def combined(sums_ref, rhs_ref, v_ref, image_ref, w_ref, second_ref, sol_ref, res_ref):
    sums = sums_ref[0]
    for s in range(1, sums_ref.shape[0]):
        sums = sums + sums_ref[s]
    rz, curv, cross, last = (sums[:CASES, n : n + 1] for n in range(4))
    step = rz / curv
    ratio = (step * step * cross - rz) / rz
    grown = 1.0 + ratio
    curv_next = grown * grown * curv - 2.0 * grown * step * cross + step * step * last
    step_next = ratio * rz / curv_next
    on_first = step + step_next * grown
    on_second = step_next * step
    v, w = v_ref[:CASES, :], w_ref[:CASES, :]
    sol = on_first * v - on_second * w
    change = on_second * second_ref[:CASES, :] - on_first * image_ref[:CASES, :]
    for c in range(CASES):
        sol_ref[c] = sol[c : c + 1]
        res_ref[c] = rhs_ref[c] + change[c : c + 1]


SMEM = pl.BlockSpec(memory_space=pltpu.SMEM)
VMEM = pl.BlockSpec(memory_space=pltpu.VMEM)


def shaped(*shape, dtype=F32):
    return jax.ShapeDtypeStruct(shape, dtype)


def in_hbm(value):
    return pltpu.with_memory_space_constraint(value, pltpu.HBM)


def call(kernel, scalars, arrays, out_shape, scratch=(), stays=0, limit=20):
    held = len(arrays) - stays
    return pl.pallas_call(
        kernel,
        in_specs=[SMEM] * len(scalars)
        + [VMEM] * held
        + [pl.BlockSpec(memory_space=pltpu.HBM)] * stays,
        out_specs=tuple(VMEM for _ in out_shape),
        out_shape=tuple(out_shape),
        scratch_shapes=list(scratch),
        compiler_params=pltpu.CompilerParams(vmem_limit_bytes=limit * MIB),
    )(*scalars, *arrays)


def body(rhs, dshift, stiff, face_k, elem_col, elem_row, face_rows):
    span = rhs.shape[2]
    face_len = FACE * BLOCK
    columns, targets = in_hbm(elem_col[0]), in_hbm(elem_row[0])
    live = in_hbm(face_rows[0])
    rhs = in_hbm(rhs.reshape(CASES, 1, span))
    dshift = in_hbm(dshift)
    core = lax.axis_index("slab_2")
    place = core.astype(jnp.int32).reshape(1)
    domains = lax.axis_size(DOM)
    slabs = lax.axis_size(SLAB)
    swap = [(0, 1), (1, 0)]
    across = [(s, (s - 1 if s % 2 == 0 else s + 1) % slabs) for s in range(slabs)]
    face = shaped(8, face_len)
    vector = shaped(8, span)

    def exchanged(near, far):
        return lax.ppermute(near, "slab_2", swap), lax.ppermute(far, SLAB, across)

    faces, face_sq = call(
        face_prep,
        [live],
        [in_hbm(face_k[0])],
        [shaped(2 * FACE, BLOCK, LANES, dtype=BF16), shaped(2, 8, face_len)],
        [pltpu.VMEM((CHUNK * 8, LANES), F32)],
    )
    sq_near, sq_far = exchanged(
        jnp.where(core == 0, face_sq[1], face_sq[0]), jnp.where(core == 0, face_sq[0], face_sq[1])
    )

    hbm = pl.BlockSpec(memory_space=pltpu.HBM)
    blocks, inner = pl.pallas_call(
        stiff_prep,
        in_specs=[SMEM, hbm],
        out_specs=(hbm, VMEM),
        out_shape=(pltpu.HBM((STORED, BLOCK, LANES), BF16), vector),
        scratch_shapes=[
            pltpu.VMEM((STORED, BLOCK * BLOCK), BF16),
            pltpu.VMEM((STORED, BLOCK, LANES), BF16),
            pltpu.VMEM((CHUNK * 16, LANES), F32),
            pltpu.VMEM((OWN, 8, LANES), F32),
            pltpu.SemaphoreType.DMA((STEPS,)),
            pltpu.SemaphoreType.DMA((STEPS,)),
        ],
        compiler_params=pltpu.CompilerParams(vmem_limit_bytes=20 * MIB),
    )(columns, in_hbm(stiff[0]))
    blocks = in_hbm(blocks)

    held = pltpu.VMEM((8, span), F32)
    cols = pltpu.VMEM((OWN, 16, LANES), BF16)
    rows = pltpu.VMEM((SLAB_ROWS, 16, LANES), BF16)
    acc = pltpu.VMEM((SLAB_ROWS, 8, LANES), F32)
    stored = [pltpu.VMEM((STORED, LANES, LANES), BF16), pltpu.SemaphoreType.DMA((STEPS,))]

    def all_rows(parts, near, far, sums=()):
        near, far = exchanged(near, far)
        parts = parts.reshape(domains, CHUNK, LANES)
        arrived = lax.all_to_all(parts, DOM, 0, 0, tiled=True)
        depth = CHUNK + 8 * len(sums)
        copies, near, far = call(
            settled,
            [place, live],
            [arrived, near, far, faces, *sums],
            [shaped(domains, depth, LANES), face, face],
            [pltpu.VMEM((CHUNK, LANES), F32)],
        )
        full = lax.all_to_all(copies, DOM, 0, 0, tiled=True)
        near, far = exchanged(near, far)
        return full, near, far

    parts, inverse, first, near, far = call(
        first_product,
        [columns, targets, place],
        [rhs, dshift, inner, sq_near, sq_far, blocks],
        [shaped(OWN * CHUNK, LANES), vector, vector, face, face],
        [held, cols, acc, *stored],
        stays=1,
    )
    full, near, far = all_rows(parts, near, far)
    parts, image, second, sums, near, far = call(
        middle_product,
        [columns, targets, place],
        [full.reshape(-1, LANES), rhs, dshift, inverse, first, near, far, blocks],
        [shaped(OWN * CHUNK, LANES), vector, vector, shaped(8, LANES), face, face],
        [held, rows, cols, acc, *stored],
        stays=1,
    )
    full, near, far = all_rows(parts, near, far, [sums])
    full, near, far = lax.optimization_barrier((full, near, far))
    sums = jnp.sum(full[:, CHUNK:], axis=0)
    sums = lax.all_to_all(
        jnp.broadcast_to(sums[None], (slabs, *sums.shape)), SLAB, 0, 0, tiled=True
    )
    (second_image,) = call(
        last_product,
        [columns, targets, place],
        [full.reshape(-1, LANES), dshift, second, near, far, blocks],
        [vector],
        [rows, pltpu.VMEM((OWN, 8, LANES), F32), *stored],
        stays=1,
    )
    out = shaped(CASES, 1, span)
    return call(combined, [], [sums, rhs, first, image, second, second_image], [out, out])


def solution(mesh):
    finer = Mesh(
        mesh.devices.reshape(4, 2, 2, 8, 2), ("slab_0", "slab_1", "slab_2", "dom_0", "dom_1")
    )
    placed = (
        P(None, SLAB, DOM),
        P(SLAB, DOM),
        P(SLAB, DOM, None),
        P(SLAB, None, DOM, None),
        P(SLAB, DOM),
        P(SLAB, DOM),
        P(SLAB, None),
    )
    return jax.shard_map(
        body,
        mesh=finer,
        in_specs=placed,
        out_specs=(P(None, SLAB, DOM), P(None, SLAB, DOM)),
        check_vma=False,
    )
```

```python
import functools

import jax
import jax.numpy as jnp
from jax import lax
from jax.experimental import pallas as pl
from jax.experimental.pallas import tpu as pltpu
from jax.sharding import Mesh
from jax.sharding import PartitionSpec as P

BLOCK = 96
CASES = 6
DOM = ("dom_0", "dom_1")
SLAB = ("slab_0", "slab_1", "slab_2")
F32 = jnp.float32
BF16 = jnp.bfloat16
LANES = 128
OWN = 16
STORED = 256
SLAB_ROWS = 256
GROUP = 32
STEPS = STORED // GROUP
CHUNK = 72
TILES = 12
FACE = 4
MIB = 1024 * 1024


def lane(rows):
    return lax.broadcasted_iota(jnp.int32, (rows, LANES), 1)


def spread(t0, t1, t2):
    at = lane(t0.shape[0])
    v0 = t0
    v1 = jnp.where(at < 32, pltpu.roll(t0, 32, 1), pltpu.roll(t1, 32, 1))
    v2 = jnp.where(at < 64, pltpu.roll(t1, 64, 1), pltpu.roll(t2, 64, 1))
    v3 = pltpu.roll(t2, 96, 1)
    return [jnp.where(at < BLOCK, v, 0.0) for v in (v0, v1, v2, v3)]


def packed(v0, v1, v2, v3):
    at = lane(v0.shape[0])
    r1 = pltpu.roll(v1, 96, 1)
    r2 = pltpu.roll(v2, 64, 1)
    r3 = pltpu.roll(v3, 32, 1)
    return (
        jnp.where(at < 96, v0, r1),
        jnp.where(at < 64, r1, r2),
        jnp.where(at < 32, r2, r3),
    )


def halves(v):
    high = v.astype(BF16).astype(F32)
    return jnp.concatenate([high, v - high], axis=0).astype(BF16)


def rows_live(shape, dim, live, block):
    at = lax.broadcasted_iota(jnp.int32, shape, dim)
    row = 4 * (at % 24) + at // 24
    return row + block * BLOCK < live


def eight(ref, start):
    if start + 8 <= ref.shape[0]:
        return ref[start : start + 8, :]
    return pltpu.roll(ref[start - 2 : start + 6, :], 6, 0)


def block_of(held, first, stride):
    parts = [held[pl.ds(first + k * (stride // 3), 24, stride=stride), :] for k in range(3)]
    return jnp.concatenate(spread(*parts), axis=0)


def face_prep(live_ref, x_ref, k_ref, sq_ref, held):
    for k in range(2):
        for t in range(CHUNK):
            held[t * 8 + k * FACE : t * 8 + (k + 1) * FACE, :] = x_ref[
                k, :, t * LANES : (t + 1) * LANES
            ].astype(F32)
    for k in range(2):
        sums = []
        for i in range(FACE):
            whole = block_of(held, k * FACE + i, 24)
            k_ref[k * FACE + i] = whole.astype(BF16)
            masked = jnp.where(rows_live((BLOCK, LANES), 0, live_ref[k], i), whole, 0.0)
            total = jnp.sum(masked * masked, axis=0, keepdims=True)
            sums.append(jnp.broadcast_to(total, (8, LANES)))
        for t, tile in enumerate(packed(*sums)):
            sq_ref[k, :, t * LANES : (t + 1) * LANES] = tile


def stiff_prep(col_ref, x_any, k_any, diag_ref, x_ref, k_ref, held, acc, came, left):
    def arriving(g):
        return pltpu.make_async_copy(x_any.at[part(g)], x_ref.at[part(g)], came.at[g])

    def leaving(g):
        return pltpu.make_async_copy(k_ref.at[part(g)], k_any.at[part(g)], left.at[g])

    for g in range(STEPS):
        arriving(g).start()
    acc[...] = jnp.zeros_like(acc)

    def group(g, carry):
        arriving(g).wait()
        for half in range(GROUP // 16):
            base = g * GROUP + half * 16
            for t in range(CHUNK):
                held[t * 16 : (t + 1) * 16, :] = x_ref[
                    pl.ds(pl.multiple_of(base, 16), 16), tile_at(t)
                ].astype(F32)
            for e in range(16):
                whole = block_of(held, e, 48)
                k_ref[base + e] = whole.astype(BF16)
                total = jnp.sum((whole * whole).reshape(12, 8, LANES), axis=0)
                j = col_ref[base + e]
                acc[j] = acc[j] + total
        leaving(g).start()
        return carry

    lax.fori_loop(0, STEPS, group, 0)
    for q in range(OWN // 4):
        sums = [
            jnp.broadcast_to(jnp.sum(acc[q * 4 + i], axis=0, keepdims=True), (8, LANES))
            for i in range(4)
        ]
        for t, tile in enumerate(packed(*sums)):
            diag_ref[:, tile_at(q * 3 + t)] = tile
    for g in range(STEPS):
        leaving(g).wait()


def tile_at(t):
    return slice(t * LANES, (t + 1) * LANES)


def part(g):
    return pl.ds(g * GROUP, GROUP)


def brought(k_any, k_ref, sems, g):
    return pltpu.make_async_copy(k_any.at[part(g)], k_ref.at[part(g), pl.ds(0, BLOCK)], sems.at[g])


def fetch(k_any, k_ref, sems):
    for g in range(STEPS):
        brought(k_any, k_ref, sems, g).start()


def fetched(k_any, k_ref, sems, g):
    brought(k_any, k_ref, sems, g).wait()


def forward(col_ref, row_ref, tiles, k_ref, out_ref, cols, acc, wait=None):
    for q in range(OWN // 4):
        for i, v in enumerate(spread(*tiles[q * 3 : q * 3 + 3])):
            cols[q * 4 + i] = halves(v)
    acc[...] = jnp.zeros_like(acc)

    def group(g, carry):
        base = g * GROUP
        if wait is not None:
            wait(g)
        for first in range(0, GROUP, 8):
            terms = []
            for e in range(first, first + 8, 2):
                x = jnp.concatenate([cols[col_ref[base + e]], cols[col_ref[base + e + 1]]], axis=0)
                two = k_ref[pl.ds(base + e, 2)].reshape(2 * LANES, LANES)
                out = lax.dot_general(
                    x, two, (((1,), (1,)), ((), ())), preferred_element_type=F32
                )
                terms.append(out[:8, :BLOCK] + out[8:16, :BLOCK])
                other = slice(LANES, LANES + BLOCK)
                terms.append(out[16:24, other] + out[24:, other])
            for e in range(first, first + 8):
                r = row_ref[base + e]
                acc[r, :, :BLOCK] = acc[r, :, :BLOCK] + terms[e - first]
        return carry

    lax.fori_loop(0, STEPS, group, 0)
    for g in range(SLAB_ROWS // 4):
        for t, tile in enumerate(packed(*[acc[g * 4 + i] for i in range(4)])):
            at = (g // 4) * CHUNK + ((g % 4) * 3 + t) * CASES
            out_ref[at : at + CASES, :] = tile[:CASES]


def adjoint(col_ref, row_ref, y_ref, k_ref, rows, acc, wait):
    depth = y_ref.shape[0] // (SLAB_ROWS // OWN)
    for g in range(SLAB_ROWS // 4):
        at = (g // 4) * depth + (g % 4) * 3 * CASES
        tiles = [eight(y_ref, at + t * CASES) for t in range(3)]
        for i, v in enumerate(spread(*tiles)):
            rows[g * 4 + i] = halves(v)
    acc[...] = jnp.zeros_like(acc)

    def group(g, carry):
        base = g * GROUP
        wait(g)
        for first in range(0, GROUP, 8):
            terms = []
            for e in range(first, first + 8, 2):
                y = jnp.concatenate([rows[row_ref[base + e]], rows[row_ref[base + e + 1]]], axis=0)
                two = jnp.concatenate([k_ref[base + e, :BLOCK], k_ref[base + e + 1, :BLOCK]], axis=1)
                out = jnp.dot(y[:, :BLOCK], two, preferred_element_type=F32)
                terms.append(out[:8, :LANES] + out[8:16, :LANES])
                terms.append(out[16:24, LANES:] + out[24:, LANES:])
            for e in range(first, first + 8):
                j = col_ref[base + e]
                acc[j] = acc[j] + terms[e - first]
        return carry

    lax.fori_loop(0, STEPS, group, 0)
    tiles = []
    for q in range(OWN // 4):
        tiles += packed(*[acc[q * 4 + i] for i in range(4)])
    return tiles


def both_sides(core, near_ref, far_ref):
    near = [near_ref[:, tile_at(t)] for t in range(3)]
    far = [far_ref[:, tile_at(t)] for t in range(3)]
    below = [jnp.where(core == 0, f, n) for n, f in zip(near, far)]
    above = [jnp.where(core == 0, n, f) for n, f in zip(near, far)]
    return below, above


def send_sides(core, lower, upper, near_ref, far_ref):
    for t in range(3):
        near_ref[:, tile_at(t)] = jnp.where(core == 0, upper[t], lower[t])
        far_ref[:, tile_at(t)] = jnp.where(core == 0, lower[t], upper[t])


def first_product(
    col_ref, row_ref, at_ref, rhs_ref, shift_ref, diag_ref, near_ref, far_ref, k_any,
    out_ref, inverse_ref, v_ref, near_out, far_out, held, cols, acc, k_ref, sems,
):
    fetch(k_any, k_ref, sems)
    core = at_ref[0]
    held[...] = jnp.zeros_like(held)
    for c in range(CASES):
        held[c : c + 1, :] = rhs_ref[c]
    below, above = both_sides(core, near_ref, far_ref)
    tiles = []
    for t in range(TILES):
        total = diag_ref[:, tile_at(t)] + shift_ref[:, tile_at(t)]
        if t < 3:
            total = total + below[t]
        if t >= 9:
            total = total + above[t - 9]
        inverse = 1.0 / total
        inverse_ref[:, tile_at(t)] = inverse
        tile = inverse * held[:, tile_at(t)]
        v_ref[:, tile_at(t)] = tile
        tiles.append(tile)
    send_sides(core, tiles[:3], tiles[9:], near_out, far_out)
    wait = functools.partial(fetched, k_any, k_ref, sems)
    forward(col_ref, row_ref, tiles, k_ref, out_ref, cols, acc, wait)


def image_tiles(core, tiles, v_ref, shift_ref, near_ref, far_ref):
    below, above = both_sides(core, near_ref, far_ref)
    whole = [
        tile + shift_ref[:, tile_at(t)] * v_ref[:, tile_at(t)] for t, tile in enumerate(tiles)
    ]
    return (
        [whole[t] + below[t] for t in range(3)]
        + whole[3:9]
        + [whole[t + 9] + above[t] for t in range(3)]
    )


def placed_sums(values):
    at = lane(8)
    out = jnp.zeros((8, LANES), F32)
    for n, value in values:
        out = jnp.where(at == n, jnp.sum(value, axis=1, keepdims=True), out)
    return out


def middle_product(
    col_ref, row_ref, at_ref, y_ref, shift_ref, inverse_ref, v_ref, near_ref, far_ref, k_any,
    out_ref, image_ref, w_ref, near_out, far_out, rows, cols, acc, k_ref, sems,
):
    fetch(k_any, k_ref, sems)
    core = at_ref[0]
    wait = functools.partial(fetched, k_any, k_ref, sems)
    tiles = adjoint(col_ref, row_ref, y_ref, k_ref, rows, acc, wait)
    tiles = image_tiles(core, tiles, v_ref, shift_ref, near_ref, far_ref)
    second = []
    for t, image in enumerate(tiles):
        image_ref[:, tile_at(t)] = image
        w = inverse_ref[:, tile_at(t)] * image
        w_ref[:, tile_at(t)] = w
        second.append(w)
    send_sides(core, second[:3], second[9:], near_out, far_out)
    forward(col_ref, row_ref, second, k_ref, out_ref, cols, acc)


def inner_products(rhs_ref, shift_ref, v_ref, image_ref, w_ref, sums_ref, held_ref):
    held_ref[...] = jnp.zeros_like(held_ref)
    for c in range(CASES):
        held_ref[c : c + 1, :] = rhs_ref[c]
    sums = [jnp.zeros((8, LANES), F32) for _ in range(4)]
    for t in range(TILES):
        v, w, image = (ref[:, tile_at(t)] for ref in (v_ref, w_ref, image_ref))
        sums[0] = sums[0] + held_ref[:, tile_at(t)] * v
        sums[1] = sums[1] + v * image
        sums[2] = sums[2] + image * w
        sums[3] = sums[3] + shift_ref[:, tile_at(t)] * w * w
    sums_ref[...] = placed_sums(enumerate(sums))


def last_product(
    col_ref, row_ref, at_ref, y_ref, shift_ref, v_ref, near_ref, far_ref, k_any,
    image_ref, rows, acc, k_ref, sems,
):
    fetch(k_any, k_ref, sems)
    wait = functools.partial(fetched, k_any, k_ref, sems)
    tiles = adjoint(col_ref, row_ref, y_ref, k_ref, rows, acc, wait)
    for t, tile in enumerate(image_tiles(at_ref[0], tiles, v_ref, shift_ref, near_ref, far_ref)):
        image_ref[:, tile_at(t)] = tile


def face_terms(at_ref, live_ref, near_ref, far_ref, k_ref, out_ref):
    for k, face in enumerate(both_sides(at_ref[0], near_ref, far_ref)):
        terms = []
        for i, v in enumerate(spread(*face)):
            out = lax.dot_general(
                halves(v), k_ref[k * FACE + i], (((1,), (1,)), ((), ())), preferred_element_type=F32
            )
            term = out[:8] + out[8:]
            term = jnp.where(rows_live((8, BLOCK), 1, live_ref[k], i), term, 0.0)
            terms.append(jnp.concatenate([term, jnp.zeros((8, LANES - BLOCK), F32)], axis=1))
        for t, tile in enumerate(packed(*terms)):
            out_ref[k, :, tile_at(t)] = tile


def settled(y_ref, terms_ref, *rest):
    out_ref, own_ref = rest[-2:]
    whole = y_ref[0]
    for d in range(1, y_ref.shape[0]):
        whole = whole + y_ref[d]
    own_ref[...] = whole
    for k in range(2):
        for t in range(3):
            at = (k * 9 + t) * CASES
            term = terms_ref[k, :, tile_at(t)]
            own_ref[at : at + CASES, :] = own_ref[at : at + CASES, :] + term[:CASES]
    own = own_ref[...]
    for d in range(out_ref.shape[0]):
        out_ref[d, :CHUNK] = own
    if len(rest) > 2:
        square = jnp.zeros((8, LANES), F32)
        for t in range(TILES):
            tile = eight(own_ref, t * CASES)
            square = square + tile * tile
        sums = rest[0][...] + placed_sums([(3, square)])
        for d in range(out_ref.shape[0]):
            out_ref[d, CHUNK:] = sums


def back_faces(at_ref, live_ref, own_ref, k_ref, near_out, far_out):
    backs = []
    for k in range(2):
        tiles = [eight(own_ref, (k * 9 + t) * CASES) for t in range(3)]
        terms = []
        for i, v in enumerate(spread(*tiles)):
            v = jnp.where(rows_live((8, LANES), 1, live_ref[k], i), v, 0.0)
            y = halves(v)
            out = jnp.dot(y[:, :BLOCK], k_ref[k * FACE + i], preferred_element_type=F32)
            terms.append(out[:8] + out[8:])
        backs.append(packed(*terms))
    send_sides(at_ref[0], backs[0], backs[1], near_out, far_out)


def combined(sums_ref, rhs_ref, v_ref, image_ref, w_ref, second_ref, sol_ref, res_ref):
    sums = sums_ref[0]
    for s in range(1, sums_ref.shape[0]):
        sums = sums + sums_ref[s]
    rz, curv, cross, last = (sums[:CASES, n : n + 1] for n in range(4))
    step = rz / curv
    ratio = (step * step * cross - rz) / rz
    grown = 1.0 + ratio
    curv_next = grown * grown * curv - 2.0 * grown * step * cross + step * step * last
    step_next = ratio * rz / curv_next
    on_first = step + step_next * grown
    on_second = step_next * step
    v, w = v_ref[:CASES, :], w_ref[:CASES, :]
    sol = on_first * v - on_second * w
    change = on_second * second_ref[:CASES, :] - on_first * image_ref[:CASES, :]
    for c in range(CASES):
        sol_ref[c] = sol[c : c + 1]
        res_ref[c] = rhs_ref[c : c + 1, :] + change[c : c + 1]


SMEM = pl.BlockSpec(memory_space=pltpu.SMEM)
VMEM = pl.BlockSpec(memory_space=pltpu.VMEM)


def shaped(*shape, dtype=F32):
    return jax.ShapeDtypeStruct(shape, dtype)


def in_hbm(value):
    return pltpu.with_memory_space_constraint(value, pltpu.HBM)


def call(kernel, scalars, arrays, out_shape, scratch=(), stays=0, limit=20):
    held = len(arrays) - stays
    return pl.pallas_call(
        kernel,
        in_specs=[SMEM] * len(scalars)
        + [VMEM] * held
        + [pl.BlockSpec(memory_space=pltpu.HBM)] * stays,
        out_specs=tuple(VMEM for _ in out_shape),
        out_shape=tuple(out_shape),
        scratch_shapes=list(scratch),
        compiler_params=pltpu.CompilerParams(vmem_limit_bytes=limit * MIB),
    )(*scalars, *arrays)


def body(rhs, dshift, stiff, face_k, elem_col, elem_row, face_rows):
    span = rhs.shape[2]
    face_len = FACE * BLOCK
    columns, targets = in_hbm(elem_col[0]), in_hbm(elem_row[0])
    live = in_hbm(face_rows[0])
    rhs = in_hbm(rhs.reshape(CASES, 1, span))
    dshift = in_hbm(dshift)
    core = lax.axis_index("slab_2")
    place = core.astype(jnp.int32).reshape(1)
    domains = lax.axis_size(DOM)
    slabs = lax.axis_size(SLAB)
    swap = [(0, 1), (1, 0)]
    across = [(s, (s - 1 if s % 2 == 0 else s + 1) % slabs) for s in range(slabs)]
    face = shaped(8, face_len)
    vector = shaped(8, span)

    def exchanged(near, far):
        return lax.ppermute(near, "slab_2", swap), lax.ppermute(far, SLAB, across)

    faces, face_sq = call(
        face_prep,
        [live],
        [in_hbm(face_k[0])],
        [shaped(2 * FACE, BLOCK, LANES, dtype=BF16), shaped(2, 8, face_len)],
        [pltpu.VMEM((CHUNK * 8, LANES), F32)],
    )
    sq_near, sq_far = exchanged(
        jnp.where(core == 0, face_sq[1], face_sq[0]), jnp.where(core == 0, face_sq[0], face_sq[1])
    )

    hbm = pl.BlockSpec(memory_space=pltpu.HBM)
    blocks, inner = pl.pallas_call(
        stiff_prep,
        in_specs=[SMEM, hbm],
        out_specs=(hbm, VMEM),
        out_shape=(pltpu.HBM((STORED, BLOCK, LANES), BF16), vector),
        scratch_shapes=[
            pltpu.VMEM((STORED, BLOCK * BLOCK), BF16),
            pltpu.VMEM((STORED, BLOCK, LANES), BF16),
            pltpu.VMEM((CHUNK * 16, LANES), F32),
            pltpu.VMEM((OWN, 8, LANES), F32),
            pltpu.SemaphoreType.DMA((STEPS,)),
            pltpu.SemaphoreType.DMA((STEPS,)),
        ],
        compiler_params=pltpu.CompilerParams(vmem_limit_bytes=20 * MIB),
    )(columns, in_hbm(stiff[0]))
    blocks = in_hbm(blocks)

    held = pltpu.VMEM((8, span), F32)
    cols = pltpu.VMEM((OWN, 16, LANES), BF16)
    rows = pltpu.VMEM((SLAB_ROWS, 16, LANES), BF16)
    acc = pltpu.VMEM((SLAB_ROWS, 8, LANES), F32)
    stored = [pltpu.VMEM((STORED, LANES, LANES), BF16), pltpu.SemaphoreType.DMA((STEPS,))]

    def all_rows(parts, near, far, sums=()):
        near, far = exchanged(near, far)
        parts = parts.reshape(domains, CHUNK, LANES)
        arrived = lax.all_to_all(parts, DOM, 0, 0, tiled=True)
        depth = CHUNK + 8 * len(sums)
        (terms,) = call(face_terms, [place, live], [near, far, faces], [shaped(2, 8, face_len)])
        copies, own = call(
            settled,
            [],
            [arrived, terms, *sums],
            [shaped(domains, depth, LANES), shaped(CHUNK, LANES)],
        )
        full = lax.all_to_all(copies, DOM, 0, 0, tiled=True)
        near, far = call(back_faces, [place, live], [own, faces], [face, face])
        near, far = exchanged(near, far)
        return full, near, far

    parts, inverse, first, near, far = call(
        first_product,
        [columns, targets, place],
        [rhs, dshift, inner, sq_near, sq_far, blocks],
        [shaped(OWN * CHUNK, LANES), vector, vector, face, face],
        [held, cols, acc, *stored],
        stays=1,
    )
    full, near, far = all_rows(parts, near, far)
    parts, image, second, near, far = call(
        middle_product,
        [columns, targets, place],
        [full.reshape(-1, LANES), dshift, inverse, first, near, far, blocks],
        [shaped(OWN * CHUNK, LANES), vector, vector, face, face],
        [rows, cols, acc, *stored],
        stays=1,
    )
    sums, whole_rhs = call(
        inner_products, [], [rhs, dshift, first, image, second], [shaped(8, LANES), vector]
    )
    full, near, far = all_rows(parts, near, far, [sums])
    full, near, far = lax.optimization_barrier((full, near, far))
    sums = jnp.sum(full[:, CHUNK:], axis=0)
    sums = lax.all_to_all(
        jnp.broadcast_to(sums[None], (slabs, *sums.shape)), SLAB, 0, 0, tiled=True
    )
    (second_image,) = call(
        last_product,
        [columns, targets, place],
        [full.reshape(-1, LANES), dshift, second, near, far, blocks],
        [vector],
        [rows, pltpu.VMEM((OWN, 8, LANES), F32), *stored],
        stays=1,
    )
    out = shaped(CASES, 1, span)
    return call(combined, [], [sums, whole_rhs, first, image, second, second_image], [out, out])


def solution(mesh):
    finer = Mesh(
        mesh.devices.reshape(4, 2, 2, 8, 2), ("slab_0", "slab_1", "slab_2", "dom_0", "dom_1")
    )
    placed = (
        P(None, SLAB, DOM),
        P(SLAB, DOM),
        P(SLAB, DOM, None),
        P(SLAB, None, DOM, None),
        P(SLAB, DOM),
        P(SLAB, DOM),
        P(SLAB, None),
    )
    return jax.shard_map(
        body,
        mesh=finer,
        in_specs=placed,
        out_specs=(P(None, SLAB, DOM), P(None, SLAB, DOM)),
        check_vma=False,
    )
```

```python
import functools

import jax
import jax.numpy as jnp
from jax import lax
from jax.experimental import pallas as pl
from jax.experimental.pallas import tpu as pltpu
from jax.sharding import Mesh
from jax.sharding import PartitionSpec as P

BLOCK = 96
CASES = 6
DOM = ("dom_0", "dom_1")
SLAB = ("slab_0", "slab_1", "slab_2")
F32 = jnp.float32
BF16 = jnp.bfloat16
LANES = 128
OWN = 16
STORED = 256
SLAB_ROWS = 256
GROUP = 32
STEPS = STORED // GROUP
CHUNK = 72
TILES = 12
FACE = 4
MIB = 1024 * 1024


def lane(rows):
    return lax.broadcasted_iota(jnp.int32, (rows, LANES), 1)


def spread(t0, t1, t2):
    at = lane(t0.shape[0])
    v0 = t0
    v1 = jnp.where(at < 32, pltpu.roll(t0, 32, 1), pltpu.roll(t1, 32, 1))
    v2 = jnp.where(at < 64, pltpu.roll(t1, 64, 1), pltpu.roll(t2, 64, 1))
    v3 = pltpu.roll(t2, 96, 1)
    return [jnp.where(at < BLOCK, v, 0.0) for v in (v0, v1, v2, v3)]


def packed(v0, v1, v2, v3):
    at = lane(v0.shape[0])
    r1 = pltpu.roll(v1, 96, 1)
    r2 = pltpu.roll(v2, 64, 1)
    r3 = pltpu.roll(v3, 32, 1)
    return (
        jnp.where(at < 96, v0, r1),
        jnp.where(at < 64, r1, r2),
        jnp.where(at < 32, r2, r3),
    )


def halves(v):
    high = v.astype(BF16).astype(F32)
    return jnp.concatenate([high, v - high], axis=0).astype(BF16)


def rows_live(shape, dim, live, block):
    at = lax.broadcasted_iota(jnp.int32, shape, dim)
    row = 4 * (at % 24) + at // 24
    return row + block * BLOCK < live


def eight(ref, start):
    if start + 8 <= ref.shape[0]:
        return ref[start : start + 8, :]
    return pltpu.roll(ref[start - 2 : start + 6, :], 6, 0)


def block_of(held, first, stride):
    parts = [held[pl.ds(first + k * (stride // 3), 24, stride=stride), :] for k in range(3)]
    return jnp.concatenate(spread(*parts), axis=0)


def face_prep(live_ref, x_ref, k_ref, sq_ref, held):
    for k in range(2):
        for t in range(CHUNK):
            held[t * 8 + k * FACE : t * 8 + (k + 1) * FACE, :] = x_ref[
                k, :, t * LANES : (t + 1) * LANES
            ].astype(F32)
    for k in range(2):
        sums = []
        for i in range(FACE):
            whole = block_of(held, k * FACE + i, 24)
            k_ref[k * FACE + i] = whole.astype(BF16)
            masked = jnp.where(rows_live((BLOCK, LANES), 0, live_ref[k], i), whole, 0.0)
            total = jnp.sum(masked * masked, axis=0, keepdims=True)
            sums.append(jnp.broadcast_to(total, (8, LANES)))
        for t, tile in enumerate(packed(*sums)):
            sq_ref[k, :, t * LANES : (t + 1) * LANES] = tile


def stiff_prep(col_ref, x_any, k_any, diag_ref, k_ref, x_ref, held, acc, came, left):
    def arriving(g):
        return pltpu.make_async_copy(x_any.at[part(g)], x_ref.at[part(g)], came.at[g])

    def leaving(g):
        return pltpu.make_async_copy(
            k_ref.at[part(g), pl.ds(0, BLOCK)], k_any.at[part(g)], left.at[g]
        )

    for g in range(STEPS):
        arriving(g).start()
    acc[...] = jnp.zeros_like(acc)

    def group(g, carry):
        arriving(g).wait()
        for half in range(GROUP // 16):
            base = g * GROUP + half * 16
            for t in range(CHUNK):
                held[t * 16 : (t + 1) * 16, :] = x_ref[
                    pl.ds(pl.multiple_of(base, 16), 16), tile_at(t)
                ].astype(F32)
            for e in range(16):
                whole = block_of(held, e, 48)
                k_ref[base + e, :BLOCK] = whole.astype(BF16)
                total = jnp.sum((whole * whole).reshape(12, 8, LANES), axis=0)
                j = col_ref[base + e]
                acc[j] = acc[j] + total
        leaving(g).start()
        return carry

    lax.fori_loop(0, STEPS, group, 0)
    for q in range(OWN // 4):
        sums = [
            jnp.broadcast_to(jnp.sum(acc[q * 4 + i], axis=0, keepdims=True), (8, LANES))
            for i in range(4)
        ]
        for t, tile in enumerate(packed(*sums)):
            diag_ref[:, tile_at(q * 3 + t)] = tile
    for g in range(STEPS):
        leaving(g).wait()


def tile_at(t):
    return slice(t * LANES, (t + 1) * LANES)


def part(g):
    return pl.ds(g * GROUP, GROUP)


def brought(k_any, k_ref, sems, g):
    return pltpu.make_async_copy(k_any.at[part(g)], k_ref.at[part(g), pl.ds(0, BLOCK)], sems.at[g])


def fetch(k_any, k_ref, sems):
    for g in range(STEPS):
        brought(k_any, k_ref, sems, g).start()


def fetched(k_any, k_ref, sems, g):
    brought(k_any, k_ref, sems, g).wait()


def forward(col_ref, row_ref, tiles, k_ref, out_ref, cols, acc, wait=None):
    for q in range(OWN // 4):
        for i, v in enumerate(spread(*tiles[q * 3 : q * 3 + 3])):
            cols[q * 4 + i] = halves(v)
    acc[...] = jnp.zeros_like(acc)

    def group(g, carry):
        base = g * GROUP
        if wait is not None:
            wait(g)
        for first in range(0, GROUP, 8):
            terms = []
            for e in range(first, first + 8, 2):
                x = jnp.concatenate([cols[col_ref[base + e]], cols[col_ref[base + e + 1]]], axis=0)
                two = k_ref[pl.ds(base + e, 2)].reshape(2 * LANES, LANES)
                out = lax.dot_general(
                    x, two, (((1,), (1,)), ((), ())), preferred_element_type=F32
                )
                terms.append(out[:8, :BLOCK] + out[8:16, :BLOCK])
                other = slice(LANES, LANES + BLOCK)
                terms.append(out[16:24, other] + out[24:, other])
            for e in range(first, first + 8):
                r = row_ref[base + e]
                acc[r, :, :BLOCK] = acc[r, :, :BLOCK] + terms[e - first]
        return carry

    lax.fori_loop(0, STEPS, group, 0)
    for g in range(SLAB_ROWS // 4):
        for t, tile in enumerate(packed(*[acc[g * 4 + i] for i in range(4)])):
            at = (g // 4) * CHUNK + ((g % 4) * 3 + t) * CASES
            out_ref[at : at + CASES, :] = tile[:CASES]


def adjoint(col_ref, row_ref, y_ref, k_ref, rows, acc, wait):
    depth = y_ref.shape[0] // (SLAB_ROWS // OWN)
    for g in range(SLAB_ROWS // 4):
        at = (g // 4) * depth + (g % 4) * 3 * CASES
        tiles = [eight(y_ref, at + t * CASES) for t in range(3)]
        for i, v in enumerate(spread(*tiles)):
            rows[g * 4 + i] = halves(v)
    acc[...] = jnp.zeros_like(acc)

    def group(g, carry):
        base = g * GROUP
        wait(g)
        for first in range(0, GROUP, 8):
            terms = []
            for e in range(first, first + 8, 2):
                y = jnp.concatenate([rows[row_ref[base + e]], rows[row_ref[base + e + 1]]], axis=0)
                two = jnp.concatenate([k_ref[base + e, :BLOCK], k_ref[base + e + 1, :BLOCK]], axis=1)
                out = jnp.dot(y[:, :BLOCK], two, preferred_element_type=F32)
                terms.append(out[:8, :LANES] + out[8:16, :LANES])
                terms.append(out[16:24, LANES:] + out[24:, LANES:])
            for e in range(first, first + 8):
                j = col_ref[base + e]
                acc[j] = acc[j] + terms[e - first]
        return carry

    lax.fori_loop(0, STEPS, group, 0)
    tiles = []
    for q in range(OWN // 4):
        tiles += packed(*[acc[q * 4 + i] for i in range(4)])
    return tiles


def both_sides(core, near_ref, far_ref):
    near = [near_ref[:, tile_at(t)] for t in range(3)]
    far = [far_ref[:, tile_at(t)] for t in range(3)]
    below = [jnp.where(core == 0, f, n) for n, f in zip(near, far)]
    above = [jnp.where(core == 0, n, f) for n, f in zip(near, far)]
    return below, above


def send_sides(core, lower, upper, near_ref, far_ref):
    for t in range(3):
        near_ref[:, tile_at(t)] = jnp.where(core == 0, upper[t], lower[t])
        far_ref[:, tile_at(t)] = jnp.where(core == 0, lower[t], upper[t])


def first_product(
    col_ref, row_ref, at_ref, rhs_ref, shift_ref, diag_ref, near_ref, far_ref, k_ref,
    out_ref, inverse_ref, v_ref, near_out, far_out, held, cols, acc,
):
    core = at_ref[0]
    held[...] = jnp.zeros_like(held)
    for c in range(CASES):
        held[c : c + 1, :] = rhs_ref[c]
    below, above = both_sides(core, near_ref, far_ref)
    tiles = []
    for t in range(TILES):
        total = diag_ref[:, tile_at(t)] + shift_ref[:, tile_at(t)]
        if t < 3:
            total = total + below[t]
        if t >= 9:
            total = total + above[t - 9]
        inverse = 1.0 / total
        inverse_ref[:, tile_at(t)] = inverse
        tile = inverse * held[:, tile_at(t)]
        v_ref[:, tile_at(t)] = tile
        tiles.append(tile)
    send_sides(core, tiles[:3], tiles[9:], near_out, far_out)
    forward(col_ref, row_ref, tiles, k_ref, out_ref, cols, acc)


def image_tiles(core, tiles, v_ref, shift_ref, near_ref, far_ref):
    below, above = both_sides(core, near_ref, far_ref)
    whole = [
        tile + shift_ref[:, tile_at(t)] * v_ref[:, tile_at(t)] for t, tile in enumerate(tiles)
    ]
    return (
        [whole[t] + below[t] for t in range(3)]
        + whole[3:9]
        + [whole[t + 9] + above[t] for t in range(3)]
    )


def placed_sums(values):
    at = lane(8)
    out = jnp.zeros((8, LANES), F32)
    for n, value in values:
        out = jnp.where(at == n, jnp.sum(value, axis=1, keepdims=True), out)
    return out


def middle_product(
    col_ref, row_ref, at_ref, y_ref, shift_ref, inverse_ref, v_ref, near_ref, far_ref, k_any,
    out_ref, image_ref, w_ref, near_out, far_out, rows, cols, acc, k_ref, sems,
):
    fetch(k_any, k_ref, sems)
    core = at_ref[0]
    wait = functools.partial(fetched, k_any, k_ref, sems)
    tiles = adjoint(col_ref, row_ref, y_ref, k_ref, rows, acc, wait)
    tiles = image_tiles(core, tiles, v_ref, shift_ref, near_ref, far_ref)
    second = []
    for t, image in enumerate(tiles):
        image_ref[:, tile_at(t)] = image
        w = inverse_ref[:, tile_at(t)] * image
        w_ref[:, tile_at(t)] = w
        second.append(w)
    send_sides(core, second[:3], second[9:], near_out, far_out)
    forward(col_ref, row_ref, second, k_ref, out_ref, cols, acc)


def inner_products(rhs_ref, shift_ref, v_ref, image_ref, w_ref, sums_ref, held_ref):
    held_ref[...] = jnp.zeros_like(held_ref)
    for c in range(CASES):
        held_ref[c : c + 1, :] = rhs_ref[c]
    sums = [jnp.zeros((8, LANES), F32) for _ in range(4)]
    for t in range(TILES):
        v, w, image = (ref[:, tile_at(t)] for ref in (v_ref, w_ref, image_ref))
        sums[0] = sums[0] + held_ref[:, tile_at(t)] * v
        sums[1] = sums[1] + v * image
        sums[2] = sums[2] + image * w
        sums[3] = sums[3] + shift_ref[:, tile_at(t)] * w * w
    sums_ref[...] = placed_sums(enumerate(sums))


def last_product(
    col_ref, row_ref, at_ref, y_ref, shift_ref, v_ref, near_ref, far_ref, k_any,
    image_ref, rows, acc, k_ref, sems,
):
    fetch(k_any, k_ref, sems)
    wait = functools.partial(fetched, k_any, k_ref, sems)
    tiles = adjoint(col_ref, row_ref, y_ref, k_ref, rows, acc, wait)
    for t, tile in enumerate(image_tiles(at_ref[0], tiles, v_ref, shift_ref, near_ref, far_ref)):
        image_ref[:, tile_at(t)] = tile


def face_terms(at_ref, live_ref, near_ref, far_ref, k_ref, out_ref):
    for k, face in enumerate(both_sides(at_ref[0], near_ref, far_ref)):
        terms = []
        for i, v in enumerate(spread(*face)):
            out = lax.dot_general(
                halves(v), k_ref[k * FACE + i], (((1,), (1,)), ((), ())), preferred_element_type=F32
            )
            term = out[:8] + out[8:]
            term = jnp.where(rows_live((8, BLOCK), 1, live_ref[k], i), term, 0.0)
            terms.append(jnp.concatenate([term, jnp.zeros((8, LANES - BLOCK), F32)], axis=1))
        for t, tile in enumerate(packed(*terms)):
            out_ref[k, :, tile_at(t)] = tile


def settled(y_ref, terms_ref, *rest):
    out_ref, own_ref = rest[-2:]
    whole = y_ref[0]
    for d in range(1, y_ref.shape[0]):
        whole = whole + y_ref[d]
    own_ref[...] = whole
    for k in range(2):
        for t in range(3):
            at = (k * 9 + t) * CASES
            term = terms_ref[k, :, tile_at(t)]
            own_ref[at : at + CASES, :] = own_ref[at : at + CASES, :] + term[:CASES]
    own = own_ref[...]
    for d in range(out_ref.shape[0]):
        out_ref[d, :CHUNK] = own
    if len(rest) > 2:
        square = jnp.zeros((8, LANES), F32)
        for t in range(TILES):
            tile = eight(own_ref, t * CASES)
            square = square + tile * tile
        sums = rest[0][...] + placed_sums([(3, square)])
        for d in range(out_ref.shape[0]):
            out_ref[d, CHUNK:] = sums


def back_faces(at_ref, live_ref, own_ref, k_ref, near_out, far_out):
    backs = []
    for k in range(2):
        tiles = [eight(own_ref, (k * 9 + t) * CASES) for t in range(3)]
        terms = []
        for i, v in enumerate(spread(*tiles)):
            v = jnp.where(rows_live((8, LANES), 1, live_ref[k], i), v, 0.0)
            y = halves(v)
            out = jnp.dot(y[:, :BLOCK], k_ref[k * FACE + i], preferred_element_type=F32)
            terms.append(out[:8] + out[8:])
        backs.append(packed(*terms))
    send_sides(at_ref[0], backs[0], backs[1], near_out, far_out)


def combined(sums_ref, rhs_ref, v_ref, image_ref, w_ref, second_ref, sol_ref, res_ref):
    sums = sums_ref[0]
    for s in range(1, sums_ref.shape[0]):
        sums = sums + sums_ref[s]
    rz, curv, cross, last = (sums[:CASES, n : n + 1] for n in range(4))
    step = rz / curv
    ratio = (step * step * cross - rz) / rz
    grown = 1.0 + ratio
    curv_next = grown * grown * curv - 2.0 * grown * step * cross + step * step * last
    step_next = ratio * rz / curv_next
    on_first = step + step_next * grown
    on_second = step_next * step
    v, w = v_ref[:CASES, :], w_ref[:CASES, :]
    sol = on_first * v - on_second * w
    change = on_second * second_ref[:CASES, :] - on_first * image_ref[:CASES, :]
    for c in range(CASES):
        sol_ref[c] = sol[c : c + 1]
        res_ref[c] = rhs_ref[c : c + 1, :] + change[c : c + 1]


SMEM = pl.BlockSpec(memory_space=pltpu.SMEM)
VMEM = pl.BlockSpec(memory_space=pltpu.VMEM)


def shaped(*shape, dtype=F32):
    return jax.ShapeDtypeStruct(shape, dtype)


def in_hbm(value):
    return pltpu.with_memory_space_constraint(value, pltpu.HBM)


def call(kernel, scalars, arrays, out_shape, scratch=(), stays=0, limit=20):
    held = len(arrays) - stays
    return pl.pallas_call(
        kernel,
        in_specs=[SMEM] * len(scalars)
        + [VMEM] * held
        + [pl.BlockSpec(memory_space=pltpu.HBM)] * stays,
        out_specs=tuple(VMEM for _ in out_shape),
        out_shape=tuple(out_shape),
        scratch_shapes=list(scratch),
        compiler_params=pltpu.CompilerParams(vmem_limit_bytes=limit * MIB),
    )(*scalars, *arrays)


def body(rhs, dshift, stiff, face_k, elem_col, elem_row, face_rows):
    span = rhs.shape[2]
    face_len = FACE * BLOCK
    columns, targets = in_hbm(elem_col[0]), in_hbm(elem_row[0])
    live = in_hbm(face_rows[0])
    rhs = in_hbm(rhs.reshape(CASES, 1, span))
    dshift = in_hbm(dshift)
    core = lax.axis_index("slab_2")
    place = core.astype(jnp.int32).reshape(1)
    domains = lax.axis_size(DOM)
    slabs = lax.axis_size(SLAB)
    swap = [(0, 1), (1, 0)]
    across = [(s, (s - 1 if s % 2 == 0 else s + 1) % slabs) for s in range(slabs)]
    face = shaped(8, face_len)
    vector = shaped(8, span)

    def exchanged(near, far):
        return lax.ppermute(near, "slab_2", swap), lax.ppermute(far, SLAB, across)

    faces, face_sq = call(
        face_prep,
        [live],
        [in_hbm(face_k[0])],
        [shaped(2 * FACE, BLOCK, LANES, dtype=BF16), shaped(2, 8, face_len)],
        [pltpu.VMEM((CHUNK * 8, LANES), F32)],
    )
    sq_near, sq_far = exchanged(
        jnp.where(core == 0, face_sq[1], face_sq[0]), jnp.where(core == 0, face_sq[0], face_sq[1])
    )

    hbm = pl.BlockSpec(memory_space=pltpu.HBM)
    blocks, inner, near_blocks = pl.pallas_call(
        stiff_prep,
        in_specs=[SMEM, hbm],
        out_specs=(hbm, VMEM, VMEM),
        out_shape=(
            pltpu.HBM((STORED, BLOCK, LANES), BF16),
            vector,
            pltpu.VMEM((STORED, LANES, LANES), BF16),
        ),
        scratch_shapes=[
            pltpu.VMEM((STORED, BLOCK * BLOCK), BF16),
            pltpu.VMEM((CHUNK * 16, LANES), F32),
            pltpu.VMEM((OWN, 8, LANES), F32),
            pltpu.SemaphoreType.DMA((STEPS,)),
            pltpu.SemaphoreType.DMA((STEPS,)),
        ],
        compiler_params=pltpu.CompilerParams(vmem_limit_bytes=20 * MIB),
    )(columns, in_hbm(stiff[0]))
    blocks = in_hbm(blocks)
    near_blocks = pltpu.with_memory_space_constraint(near_blocks, pltpu.VMEM)

    held = pltpu.VMEM((8, span), F32)
    cols = pltpu.VMEM((OWN, 16, LANES), BF16)
    rows = pltpu.VMEM((SLAB_ROWS, 16, LANES), BF16)
    acc = pltpu.VMEM((SLAB_ROWS, 8, LANES), F32)
    stored = [pltpu.VMEM((STORED, LANES, LANES), BF16), pltpu.SemaphoreType.DMA((STEPS,))]

    def all_rows(parts, near, far, sums=()):
        near, far = exchanged(near, far)
        parts = parts.reshape(domains, CHUNK, LANES)
        arrived = lax.all_to_all(parts, DOM, 0, 0, tiled=True)
        depth = CHUNK + 8 * len(sums)
        (terms,) = call(face_terms, [place, live], [near, far, faces], [shaped(2, 8, face_len)])
        copies, own = call(
            settled,
            [],
            [arrived, terms, *sums],
            [shaped(domains, depth, LANES), shaped(CHUNK, LANES)],
        )
        full = lax.all_to_all(copies, DOM, 0, 0, tiled=True)
        near, far = call(back_faces, [place, live], [own, faces], [face, face])
        near, far = exchanged(near, far)
        return full, near, far

    parts, inverse, first, near, far = call(
        first_product,
        [columns, targets, place],
        [rhs, dshift, inner, sq_near, sq_far, near_blocks],
        [shaped(OWN * CHUNK, LANES), vector, vector, face, face],
        [held, cols, acc],
    )
    full, near, far = all_rows(parts, near, far)
    parts, image, second, near, far = call(
        middle_product,
        [columns, targets, place],
        [full.reshape(-1, LANES), dshift, inverse, first, near, far, blocks],
        [shaped(OWN * CHUNK, LANES), vector, vector, face, face],
        [rows, cols, acc, *stored],
        stays=1,
    )
    sums, whole_rhs = call(
        inner_products, [], [rhs, dshift, first, image, second], [shaped(8, LANES), vector]
    )
    full, near, far = all_rows(parts, near, far, [sums])
    full, near, far = lax.optimization_barrier((full, near, far))
    sums = jnp.sum(full[:, CHUNK:], axis=0)
    sums = lax.all_to_all(
        jnp.broadcast_to(sums[None], (slabs, *sums.shape)), SLAB, 0, 0, tiled=True
    )
    (second_image,) = call(
        last_product,
        [columns, targets, place],
        [full.reshape(-1, LANES), dshift, second, near, far, blocks],
        [vector],
        [rows, pltpu.VMEM((OWN, 8, LANES), F32), *stored],
        stays=1,
    )
    out = shaped(CASES, 1, span)
    return call(combined, [], [sums, whole_rhs, first, image, second, second_image], [out, out])


def solution(mesh):
    finer = Mesh(
        mesh.devices.reshape(4, 2, 2, 8, 2), ("slab_0", "slab_1", "slab_2", "dom_0", "dom_1")
    )
    placed = (
        P(None, SLAB, DOM),
        P(SLAB, DOM),
        P(SLAB, DOM, None),
        P(SLAB, None, DOM, None),
        P(SLAB, DOM),
        P(SLAB, DOM),
        P(SLAB, None),
    )
    return jax.shard_map(
        body,
        mesh=finer,
        in_specs=placed,
        out_specs=(P(None, SLAB, DOM), P(None, SLAB, DOM)),
        check_vma=False,
    )
```

```python
import functools

import jax
import jax.numpy as jnp
from jax import lax
from jax.experimental import pallas as pl
from jax.experimental.pallas import tpu as pltpu
from jax.sharding import Mesh
from jax.sharding import PartitionSpec as P

BLOCK = 96
CASES = 6
DOM = ("dom_0", "dom_1")
SLAB = ("slab_0", "slab_1", "slab_2")
F32 = jnp.float32
BF16 = jnp.bfloat16
LANES = 128
OWN = 16
STORED = 256
SLAB_ROWS = 256
GROUP = 64
STEPS = STORED // GROUP
CHUNK = 72
TILES = 12
PITCH = 17
FACE = 4
MIB = 1024 * 1024


def lane(rows):
    return lax.broadcasted_iota(jnp.int32, (rows, LANES), 1)


def spread(t0, t1, t2):
    at = lane(t0.shape[0])
    v0 = t0
    v1 = jnp.where(at < 32, pltpu.roll(t0, 32, 1), pltpu.roll(t1, 32, 1))
    v2 = jnp.where(at < 64, pltpu.roll(t1, 64, 1), pltpu.roll(t2, 64, 1))
    v3 = pltpu.roll(t2, 96, 1)
    return [jnp.where(at < BLOCK, v, 0.0) for v in (v0, v1, v2, v3)]


def packed(v0, v1, v2, v3):
    at = lane(v0.shape[0])
    r1 = pltpu.roll(v1, 96, 1)
    r2 = pltpu.roll(v2, 64, 1)
    r3 = pltpu.roll(v3, 32, 1)
    return (
        jnp.where(at < 96, v0, r1),
        jnp.where(at < 64, r1, r2),
        jnp.where(at < 32, r2, r3),
    )


def halves(v):
    high = v.astype(BF16).astype(F32)
    return jnp.concatenate([high, v - high], axis=0).astype(BF16)


def rows_live(shape, dim, live, block):
    at = lax.broadcasted_iota(jnp.int32, shape, dim)
    row = 4 * (at % 24) + at // 24
    return row + block * BLOCK < live


def eight(ref, start):
    if start + 8 <= ref.shape[0]:
        return ref[start : start + 8, :]
    return pltpu.roll(ref[start - 2 : start + 6, :], 6, 0)


def block_of(held, first, stride):
    parts = [held[pl.ds(first + k * (stride // 3), 24, stride=stride), :] for k in range(3)]
    return jnp.concatenate(spread(*parts), axis=0)


def face_prep(live_ref, x_ref, k_ref, sq_ref, held):
    for k in range(2):
        for t in range(CHUNK):
            held[t * 8 + k * FACE : t * 8 + (k + 1) * FACE, :] = x_ref[
                k, :, t * LANES : (t + 1) * LANES
            ].astype(F32)
    for k in range(2):
        sums = []
        for i in range(FACE):
            whole = block_of(held, k * FACE + i, 24)
            k_ref[k * FACE + i] = whole.astype(BF16)
            masked = jnp.where(rows_live((BLOCK, LANES), 0, live_ref[k], i), whole, 0.0)
            total = jnp.sum(masked * masked, axis=0, keepdims=True)
            sums.append(jnp.broadcast_to(total, (8, LANES)))
        for t, tile in enumerate(packed(*sums)):
            sq_ref[k, :, t * LANES : (t + 1) * LANES] = tile


def stiff_prep(col_ref, x_any, k_any, diag_ref, k_ref, x_ref, held, acc, came, left):
    def arriving(g):
        return pltpu.make_async_copy(x_any.at[part(g)], x_ref.at[part(g)], came.at[g])

    def leaving(g):
        return pltpu.make_async_copy(
            k_ref.at[part(g), pl.ds(0, BLOCK)], k_any.at[part(g)], left.at[g]
        )

    for g in range(STEPS):
        arriving(g).start()
    acc[...] = jnp.zeros_like(acc)

    def group(g, carry):
        arriving(g).wait()
        for half in range(GROUP // 16):
            base = g * GROUP + half * 16
            for t in range(CHUNK):
                held[t * PITCH : t * PITCH + 16, :] = x_ref[
                    pl.ds(pl.multiple_of(base, 16), 16), tile_at(t)
                ].astype(F32)
            for e in range(16):
                whole = block_of(held, e, 3 * PITCH)
                k_ref[base + e, :BLOCK] = whole.astype(BF16)
                total = jnp.sum((whole * whole).reshape(12, 8, LANES), axis=0)
                j = col_ref[base + e]
                acc[j] = acc[j] + total
        leaving(g).start()
        return carry

    lax.fori_loop(0, STEPS, group, 0)
    for q in range(OWN // 4):
        sums = [
            jnp.broadcast_to(jnp.sum(acc[q * 4 + i], axis=0, keepdims=True), (8, LANES))
            for i in range(4)
        ]
        for t, tile in enumerate(packed(*sums)):
            diag_ref[:, tile_at(q * 3 + t)] = tile
    for g in range(STEPS):
        leaving(g).wait()


def tile_at(t):
    return slice(t * LANES, (t + 1) * LANES)


def part(g):
    return pl.ds(g * GROUP, GROUP)


def brought(k_any, k_ref, sems, g):
    return pltpu.make_async_copy(k_any.at[part(g)], k_ref.at[part(g), pl.ds(0, BLOCK)], sems.at[g])


def fetch(k_any, k_ref, sems):
    for g in range(STEPS):
        brought(k_any, k_ref, sems, g).start()


def fetched(k_any, k_ref, sems, g):
    brought(k_any, k_ref, sems, g).wait()


def forward(col_ref, row_ref, tiles, k_ref, out_ref, cols, acc, wait=None):
    for q in range(OWN // 4):
        for i, v in enumerate(spread(*tiles[q * 3 : q * 3 + 3])):
            cols[q * 4 + i] = halves(v)
    acc[...] = jnp.zeros_like(acc)

    def group(g, carry):
        base = g * GROUP
        if wait is not None:
            wait(g)
        for first in range(0, GROUP, 8):
            terms = []
            for e in range(first, first + 8, 2):
                x = jnp.concatenate([cols[col_ref[base + e]], cols[col_ref[base + e + 1]]], axis=0)
                two = k_ref[pl.ds(base + e, 2)].reshape(2 * LANES, LANES)
                out = lax.dot_general(
                    x, two, (((1,), (1,)), ((), ())), preferred_element_type=F32
                )
                terms.append(out[:8, :BLOCK] + out[8:16, :BLOCK])
                other = slice(LANES, LANES + BLOCK)
                terms.append(out[16:24, other] + out[24:, other])
            for e in range(first, first + 8):
                r = row_ref[base + e]
                acc[r, :, :BLOCK] = acc[r, :, :BLOCK] + terms[e - first]
        return carry

    lax.fori_loop(0, STEPS, group, 0)
    for g in range(SLAB_ROWS // 4):
        for t, tile in enumerate(packed(*[acc[g * 4 + i] for i in range(4)])):
            at = (g // 4) * CHUNK + ((g % 4) * 3 + t) * CASES
            out_ref[at : at + CASES, :] = tile[:CASES]


def adjoint(col_ref, row_ref, y_ref, k_ref, rows, acc, wait):
    depth = y_ref.shape[0] // (SLAB_ROWS // OWN)
    for g in range(SLAB_ROWS // 4):
        at = (g // 4) * depth + (g % 4) * 3 * CASES
        tiles = [eight(y_ref, at + t * CASES) for t in range(3)]
        for i, v in enumerate(spread(*tiles)):
            rows[g * 4 + i] = halves(v)
    acc[...] = jnp.zeros_like(acc)

    def group(g, carry):
        base = g * GROUP
        wait(g)
        for first in range(0, GROUP, 8):
            terms = []
            for e in range(first, first + 8, 2):
                y = jnp.concatenate([rows[row_ref[base + e]], rows[row_ref[base + e + 1]]], axis=0)
                two = jnp.concatenate([k_ref[base + e, :BLOCK], k_ref[base + e + 1, :BLOCK]], axis=1)
                out = jnp.dot(y[:, :BLOCK], two, preferred_element_type=F32)
                terms.append(out[:8, :LANES] + out[8:16, :LANES])
                terms.append(out[16:24, LANES:] + out[24:, LANES:])
            for e in range(first, first + 8):
                j = col_ref[base + e]
                acc[j] = acc[j] + terms[e - first]
        return carry

    lax.fori_loop(0, STEPS, group, 0)
    tiles = []
    for q in range(OWN // 4):
        tiles += packed(*[acc[q * 4 + i] for i in range(4)])
    return tiles


def both_sides(core, near_ref, far_ref):
    near = [near_ref[:, tile_at(t)] for t in range(3)]
    far = [far_ref[:, tile_at(t)] for t in range(3)]
    below = [jnp.where(core == 0, f, n) for n, f in zip(near, far)]
    above = [jnp.where(core == 0, n, f) for n, f in zip(near, far)]
    return below, above


def send_sides(core, lower, upper, near_ref, far_ref):
    for t in range(3):
        near_ref[:, tile_at(t)] = jnp.where(core == 0, upper[t], lower[t])
        far_ref[:, tile_at(t)] = jnp.where(core == 0, lower[t], upper[t])


def first_product(
    col_ref, row_ref, at_ref, rhs_ref, shift_ref, diag_ref, near_ref, far_ref, k_ref,
    out_ref, inverse_ref, v_ref, near_out, far_out, held, cols, acc,
):
    core = at_ref[0]
    held[...] = jnp.zeros_like(held)
    for c in range(CASES):
        held[c : c + 1, :] = rhs_ref[c]
    below, above = both_sides(core, near_ref, far_ref)
    tiles = []
    for t in range(TILES):
        total = diag_ref[:, tile_at(t)] + shift_ref[:, tile_at(t)]
        if t < 3:
            total = total + below[t]
        if t >= 9:
            total = total + above[t - 9]
        inverse = 1.0 / total
        inverse_ref[:, tile_at(t)] = inverse
        tile = inverse * held[:, tile_at(t)]
        v_ref[:, tile_at(t)] = tile
        tiles.append(tile)
    send_sides(core, tiles[:3], tiles[9:], near_out, far_out)
    forward(col_ref, row_ref, tiles, k_ref, out_ref, cols, acc)


def image_tiles(core, tiles, v_ref, shift_ref, near_ref, far_ref):
    below, above = both_sides(core, near_ref, far_ref)
    whole = [
        tile + shift_ref[:, tile_at(t)] * v_ref[:, tile_at(t)] for t, tile in enumerate(tiles)
    ]
    return (
        [whole[t] + below[t] for t in range(3)]
        + whole[3:9]
        + [whole[t + 9] + above[t] for t in range(3)]
    )


def placed_sums(values):
    at = lane(8)
    out = jnp.zeros((8, LANES), F32)
    for n, value in values:
        out = jnp.where(at == n, jnp.sum(value, axis=1, keepdims=True), out)
    return out


def middle_product(
    col_ref, row_ref, at_ref, y_ref, shift_ref, inverse_ref, v_ref, near_ref, far_ref, k_any,
    out_ref, image_ref, w_ref, near_out, far_out, rows, cols, acc, k_ref, sems,
):
    fetch(k_any, k_ref, sems)
    core = at_ref[0]
    wait = functools.partial(fetched, k_any, k_ref, sems)
    tiles = adjoint(col_ref, row_ref, y_ref, k_ref, rows, acc, wait)
    tiles = image_tiles(core, tiles, v_ref, shift_ref, near_ref, far_ref)
    second = []
    for t, image in enumerate(tiles):
        image_ref[:, tile_at(t)] = image
        w = inverse_ref[:, tile_at(t)] * image
        w_ref[:, tile_at(t)] = w
        second.append(w)
    send_sides(core, second[:3], second[9:], near_out, far_out)
    forward(col_ref, row_ref, second, k_ref, out_ref, cols, acc)


def inner_products(rhs_ref, shift_ref, v_ref, image_ref, w_ref, sums_ref, held_ref):
    held_ref[...] = jnp.zeros_like(held_ref)
    for c in range(CASES):
        held_ref[c : c + 1, :] = rhs_ref[c]
    sums = [jnp.zeros((8, LANES), F32) for _ in range(4)]
    for t in range(TILES):
        v, w, image = (ref[:, tile_at(t)] for ref in (v_ref, w_ref, image_ref))
        sums[0] = sums[0] + held_ref[:, tile_at(t)] * v
        sums[1] = sums[1] + v * image
        sums[2] = sums[2] + image * w
        sums[3] = sums[3] + shift_ref[:, tile_at(t)] * w * w
    sums_ref[...] = placed_sums(enumerate(sums))


def last_product(
    col_ref, row_ref, at_ref, y_ref, shift_ref, v_ref, near_ref, far_ref, k_any,
    image_ref, rows, acc, k_ref, sems,
):
    fetch(k_any, k_ref, sems)
    wait = functools.partial(fetched, k_any, k_ref, sems)
    tiles = adjoint(col_ref, row_ref, y_ref, k_ref, rows, acc, wait)
    for t, tile in enumerate(image_tiles(at_ref[0], tiles, v_ref, shift_ref, near_ref, far_ref)):
        image_ref[:, tile_at(t)] = tile


def face_terms(at_ref, live_ref, near_ref, far_ref, k_ref, out_ref):
    for k, face in enumerate(both_sides(at_ref[0], near_ref, far_ref)):
        terms = []
        for i, v in enumerate(spread(*face)):
            out = lax.dot_general(
                halves(v), k_ref[k * FACE + i], (((1,), (1,)), ((), ())), preferred_element_type=F32
            )
            term = out[:8] + out[8:]
            term = jnp.where(rows_live((8, BLOCK), 1, live_ref[k], i), term, 0.0)
            terms.append(jnp.concatenate([term, jnp.zeros((8, LANES - BLOCK), F32)], axis=1))
        for t, tile in enumerate(packed(*terms)):
            out_ref[k, :, tile_at(t)] = tile


def settled(y_ref, terms_ref, *rest):
    out_ref, own_ref = rest[-2:]
    whole = y_ref[0]
    for d in range(1, y_ref.shape[0]):
        whole = whole + y_ref[d]
    own_ref[...] = whole
    for k in range(2):
        for t in range(3):
            at = (k * 9 + t) * CASES
            term = terms_ref[k, :, tile_at(t)]
            own_ref[at : at + CASES, :] = own_ref[at : at + CASES, :] + term[:CASES]
    own = own_ref[...]
    for d in range(out_ref.shape[0]):
        out_ref[d, :CHUNK] = own
    if len(rest) > 2:
        square = jnp.zeros((8, LANES), F32)
        for t in range(TILES):
            tile = eight(own_ref, t * CASES)
            square = square + tile * tile
        sums = rest[0][...] + placed_sums([(3, square)])
        for d in range(out_ref.shape[0]):
            out_ref[d, CHUNK:] = sums


def back_faces(at_ref, live_ref, own_ref, k_ref, near_out, far_out):
    backs = []
    for k in range(2):
        tiles = [eight(own_ref, (k * 9 + t) * CASES) for t in range(3)]
        terms = []
        for i, v in enumerate(spread(*tiles)):
            v = jnp.where(rows_live((8, LANES), 1, live_ref[k], i), v, 0.0)
            y = halves(v)
            out = jnp.dot(y[:, :BLOCK], k_ref[k * FACE + i], preferred_element_type=F32)
            terms.append(out[:8] + out[8:])
        backs.append(packed(*terms))
    send_sides(at_ref[0], backs[0], backs[1], near_out, far_out)


def combined(sums_ref, rhs_ref, v_ref, image_ref, w_ref, second_ref, sol_ref, res_ref):
    sums = sums_ref[0]
    for s in range(1, sums_ref.shape[0]):
        sums = sums + sums_ref[s]
    rz, curv, cross, last = (sums[:CASES, n : n + 1] for n in range(4))
    step = rz / curv
    ratio = (step * step * cross - rz) / rz
    grown = 1.0 + ratio
    curv_next = grown * grown * curv - 2.0 * grown * step * cross + step * step * last
    step_next = ratio * rz / curv_next
    on_first = step + step_next * grown
    on_second = step_next * step
    v, w = v_ref[:CASES, :], w_ref[:CASES, :]
    sol = on_first * v - on_second * w
    change = on_second * second_ref[:CASES, :] - on_first * image_ref[:CASES, :]
    for c in range(CASES):
        sol_ref[c] = sol[c : c + 1]
        res_ref[c] = rhs_ref[c : c + 1, :] + change[c : c + 1]


SMEM = pl.BlockSpec(memory_space=pltpu.SMEM)
VMEM = pl.BlockSpec(memory_space=pltpu.VMEM)


def shaped(*shape, dtype=F32):
    return jax.ShapeDtypeStruct(shape, dtype)


def in_hbm(value):
    return pltpu.with_memory_space_constraint(value, pltpu.HBM)


def call(kernel, scalars, arrays, out_shape, scratch=(), stays=0, limit=20):
    held = len(arrays) - stays
    return pl.pallas_call(
        kernel,
        in_specs=[SMEM] * len(scalars)
        + [VMEM] * held
        + [pl.BlockSpec(memory_space=pltpu.HBM)] * stays,
        out_specs=tuple(VMEM for _ in out_shape),
        out_shape=tuple(out_shape),
        scratch_shapes=list(scratch),
        compiler_params=pltpu.CompilerParams(vmem_limit_bytes=limit * MIB),
    )(*scalars, *arrays)


def body(rhs, dshift, stiff, face_k, elem_col, elem_row, face_rows):
    span = rhs.shape[2]
    face_len = FACE * BLOCK
    columns, targets = in_hbm(elem_col[0]), in_hbm(elem_row[0])
    live = in_hbm(face_rows[0])
    rhs = in_hbm(rhs.reshape(CASES, 1, span))
    dshift = in_hbm(dshift)
    core = lax.axis_index("slab_2")
    place = core.astype(jnp.int32).reshape(1)
    domains = lax.axis_size(DOM)
    slabs = lax.axis_size(SLAB)
    swap = [(0, 1), (1, 0)]
    across = [(s, (s - 1 if s % 2 == 0 else s + 1) % slabs) for s in range(slabs)]
    face = shaped(8, face_len)
    vector = shaped(8, span)

    def exchanged(near, far):
        return lax.ppermute(near, "slab_2", swap), lax.ppermute(far, SLAB, across)

    faces, face_sq = call(
        face_prep,
        [live],
        [in_hbm(face_k[0])],
        [shaped(2 * FACE, BLOCK, LANES, dtype=BF16), shaped(2, 8, face_len)],
        [pltpu.VMEM((CHUNK * 8, LANES), F32)],
    )
    sq_near, sq_far = exchanged(
        jnp.where(core == 0, face_sq[1], face_sq[0]), jnp.where(core == 0, face_sq[0], face_sq[1])
    )

    hbm = pl.BlockSpec(memory_space=pltpu.HBM)
    blocks, inner, near_blocks = pl.pallas_call(
        stiff_prep,
        in_specs=[SMEM, hbm],
        out_specs=(hbm, VMEM, VMEM),
        out_shape=(
            pltpu.HBM((STORED, BLOCK, LANES), BF16),
            vector,
            pltpu.VMEM((STORED, LANES, LANES), BF16),
        ),
        scratch_shapes=[
            pltpu.VMEM((STORED, BLOCK * BLOCK), BF16),
            pltpu.VMEM((CHUNK * PITCH, LANES), F32),
            pltpu.VMEM((OWN, 8, LANES), F32),
            pltpu.SemaphoreType.DMA((STEPS,)),
            pltpu.SemaphoreType.DMA((STEPS,)),
        ],
        compiler_params=pltpu.CompilerParams(vmem_limit_bytes=20 * MIB),
    )(columns, in_hbm(stiff[0]))
    blocks = in_hbm(blocks)
    near_blocks = pltpu.with_memory_space_constraint(near_blocks, pltpu.VMEM)

    held = pltpu.VMEM((8, span), F32)
    cols = pltpu.VMEM((OWN, 16, LANES), BF16)
    rows = pltpu.VMEM((SLAB_ROWS, 16, LANES), BF16)
    acc = pltpu.VMEM((SLAB_ROWS, 8, LANES), F32)
    stored = [pltpu.VMEM((STORED, LANES, LANES), BF16), pltpu.SemaphoreType.DMA((STEPS,))]

    def all_rows(parts, near, far, sums=()):
        near, far = exchanged(near, far)
        parts = parts.reshape(domains, CHUNK, LANES)
        arrived = lax.all_to_all(parts, DOM, 0, 0, tiled=True)
        depth = CHUNK + 8 * len(sums)
        (terms,) = call(face_terms, [place, live], [near, far, faces], [shaped(2, 8, face_len)])
        copies, own = call(
            settled,
            [],
            [arrived, terms, *sums],
            [shaped(domains, depth, LANES), shaped(CHUNK, LANES)],
        )
        full = lax.all_to_all(copies, DOM, 0, 0, tiled=True)
        near, far = call(back_faces, [place, live], [own, faces], [face, face])
        near, far = exchanged(near, far)
        return full, near, far

    parts, inverse, first, near, far = call(
        first_product,
        [columns, targets, place],
        [rhs, dshift, inner, sq_near, sq_far, near_blocks],
        [shaped(OWN * CHUNK, LANES), vector, vector, face, face],
        [held, cols, acc],
    )
    full, near, far = all_rows(parts, near, far)
    parts, image, second, near, far = call(
        middle_product,
        [columns, targets, place],
        [full.reshape(-1, LANES), dshift, inverse, first, near, far, blocks],
        [shaped(OWN * CHUNK, LANES), vector, vector, face, face],
        [rows, cols, acc, *stored],
        stays=1,
    )
    sums, whole_rhs = call(
        inner_products, [], [rhs, dshift, first, image, second], [shaped(8, LANES), vector]
    )
    full, near, far = all_rows(parts, near, far, [sums])
    full, near, far = lax.optimization_barrier((full, near, far))
    sums = jnp.sum(full[:, CHUNK:], axis=0)
    sums = lax.all_to_all(
        jnp.broadcast_to(sums[None], (slabs, *sums.shape)), SLAB, 0, 0, tiled=True
    )
    (second_image,) = call(
        last_product,
        [columns, targets, place],
        [full.reshape(-1, LANES), dshift, second, near, far, blocks],
        [vector],
        [rows, pltpu.VMEM((OWN, 8, LANES), F32), *stored],
        stays=1,
    )
    out = shaped(CASES, 1, span)
    return call(combined, [], [sums, whole_rhs, first, image, second, second_image], [out, out])


def solution(mesh):
    finer = Mesh(
        mesh.devices.reshape(4, 2, 2, 8, 2), ("slab_0", "slab_1", "slab_2", "dom_0", "dom_1")
    )
    placed = (
        P(None, SLAB, DOM),
        P(SLAB, DOM),
        P(SLAB, DOM, None),
        P(SLAB, None, DOM, None),
        P(SLAB, DOM),
        P(SLAB, DOM),
        P(SLAB, None),
    )
    return jax.shard_map(
        body,
        mesh=finer,
        in_specs=placed,
        out_specs=(P(None, SLAB, DOM), P(None, SLAB, DOM)),
        check_vma=False,
    )
```

```python
import functools

import jax
import jax.numpy as jnp
from jax import lax
from jax.experimental import pallas as pl
from jax.experimental.pallas import tpu as pltpu
from jax.sharding import Mesh
from jax.sharding import PartitionSpec as P

BLOCK = 96
CASES = 6
DOM = ("dom_0", "dom_1")
SLAB = ("slab_0", "slab_1", "slab_2")
F32 = jnp.float32
BF16 = jnp.bfloat16
LANES = 128
OWN = 16
STORED = 256
SLAB_ROWS = 256
GROUP = 128
STEPS = STORED // GROUP
CHUNK = 72
TILES = 12
PITCH = 17
FACE = 4
MIB = 1024 * 1024


def lane(rows):
    return lax.broadcasted_iota(jnp.int32, (rows, LANES), 1)


def spread(t0, t1, t2):
    at = lane(t0.shape[0])
    v0 = t0
    v1 = jnp.where(at < 32, pltpu.roll(t0, 32, 1), pltpu.roll(t1, 32, 1))
    v2 = jnp.where(at < 64, pltpu.roll(t1, 64, 1), pltpu.roll(t2, 64, 1))
    v3 = pltpu.roll(t2, 96, 1)
    return [jnp.where(at < BLOCK, v, 0.0) for v in (v0, v1, v2, v3)]


def packed(v0, v1, v2, v3):
    at = lane(v0.shape[0])
    r1 = pltpu.roll(v1, 96, 1)
    r2 = pltpu.roll(v2, 64, 1)
    r3 = pltpu.roll(v3, 32, 1)
    return (
        jnp.where(at < 96, v0, r1),
        jnp.where(at < 64, r1, r2),
        jnp.where(at < 32, r2, r3),
    )


def halves(v):
    high = v.astype(BF16).astype(F32)
    return jnp.concatenate([high, v - high], axis=0).astype(BF16)


def rows_live(shape, dim, live, block):
    at = lax.broadcasted_iota(jnp.int32, shape, dim)
    row = 4 * (at % 24) + at // 24
    return row + block * BLOCK < live


def eight(ref, start):
    if start + 8 <= ref.shape[0]:
        return ref[start : start + 8, :]
    return pltpu.roll(ref[start - 2 : start + 6, :], 6, 0)


def block_of(held, first, stride):
    parts = [held[pl.ds(first + k * (stride // 3), 24, stride=stride), :] for k in range(3)]
    return jnp.concatenate(spread(*parts), axis=0)


def face_prep(live_ref, x_ref, k_ref, sq_ref, held):
    for k in range(2):
        for t in range(CHUNK):
            held[t * 8 + k * FACE : t * 8 + (k + 1) * FACE, :] = x_ref[
                k, :, t * LANES : (t + 1) * LANES
            ].astype(F32)
    for k in range(2):
        sums = []
        for i in range(FACE):
            whole = block_of(held, k * FACE + i, 24)
            k_ref[k * FACE + i] = whole.astype(BF16)
            masked = jnp.where(rows_live((BLOCK, LANES), 0, live_ref[k], i), whole, 0.0)
            total = jnp.sum(masked * masked, axis=0, keepdims=True)
            sums.append(jnp.broadcast_to(total, (8, LANES)))
        for t, tile in enumerate(packed(*sums)):
            sq_ref[k, :, t * LANES : (t + 1) * LANES] = tile


def stiff_prep(col_ref, x_any, k_any, diag_ref, k_ref, x_ref, held, acc, came, left):
    def arriving(g):
        return pltpu.make_async_copy(x_any.at[part(g)], x_ref.at[part(g)], came.at[g])

    def leaving(g):
        return pltpu.make_async_copy(
            k_ref.at[part(g), pl.ds(0, BLOCK)], k_any.at[part(g)], left.at[g]
        )

    for g in range(STEPS):
        arriving(g).start()
    acc[...] = jnp.zeros_like(acc)

    def group(g, carry):
        arriving(g).wait()
        for half in range(GROUP // 16):
            base = g * GROUP + half * 16
            for t in range(CHUNK):
                held[t * PITCH : t * PITCH + 16, :] = x_ref[
                    pl.ds(pl.multiple_of(base, 16), 16), tile_at(t)
                ].astype(F32)
            for e in range(16):
                whole = block_of(held, e, 3 * PITCH)
                k_ref[base + e, :BLOCK] = whole.astype(BF16)
                total = jnp.sum((whole * whole).reshape(12, 8, LANES), axis=0)
                j = col_ref[base + e]
                acc[j] = acc[j] + total
        leaving(g).start()
        return carry

    lax.fori_loop(0, STEPS, group, 0)
    for q in range(OWN // 4):
        sums = [
            jnp.broadcast_to(jnp.sum(acc[q * 4 + i], axis=0, keepdims=True), (8, LANES))
            for i in range(4)
        ]
        for t, tile in enumerate(packed(*sums)):
            diag_ref[:, tile_at(q * 3 + t)] = tile
    for g in range(STEPS):
        leaving(g).wait()


def tile_at(t):
    return slice(t * LANES, (t + 1) * LANES)


def part(g):
    return pl.ds(g * GROUP, GROUP)


def brought(k_any, k_ref, sems, g):
    return pltpu.make_async_copy(k_any.at[part(g)], k_ref.at[part(g), pl.ds(0, BLOCK)], sems.at[g])


def fetch(k_any, k_ref, sems):
    for g in range(STEPS):
        brought(k_any, k_ref, sems, g).start()


def fetched(k_any, k_ref, sems, g):
    brought(k_any, k_ref, sems, g).wait()


def forward(col_ref, row_ref, tiles, k_ref, out_ref, cols, acc, wait=None):
    for q in range(OWN // 4):
        for i, v in enumerate(spread(*tiles[q * 3 : q * 3 + 3])):
            cols[q * 4 + i] = halves(v)
    acc[...] = jnp.zeros_like(acc)

    def group(g, carry):
        base = g * GROUP
        if wait is not None:
            wait(g)
        for first in range(0, GROUP, 8):
            terms = []
            for e in range(first, first + 8, 2):
                x = jnp.concatenate([cols[col_ref[base + e]], cols[col_ref[base + e + 1]]], axis=0)
                two = k_ref[pl.ds(base + e, 2)].reshape(2 * LANES, LANES)
                out = lax.dot_general(
                    x, two, (((1,), (1,)), ((), ())), preferred_element_type=F32
                )
                terms.append(out[:8, :BLOCK] + out[8:16, :BLOCK])
                other = slice(LANES, LANES + BLOCK)
                terms.append(out[16:24, other] + out[24:, other])
            for e in range(first, first + 8):
                r = row_ref[base + e]
                acc[r, :, :BLOCK] = acc[r, :, :BLOCK] + terms[e - first]
        return carry

    lax.fori_loop(0, STEPS, group, 0)
    for g in range(SLAB_ROWS // 4):
        for t, tile in enumerate(packed(*[acc[g * 4 + i] for i in range(4)])):
            at = (g // 4) * CHUNK + ((g % 4) * 3 + t) * CASES
            out_ref[at : at + CASES, :] = tile[:CASES]


def adjoint(col_ref, row_ref, y_ref, k_ref, rows, acc, wait):
    depth = y_ref.shape[0] // (SLAB_ROWS // OWN)
    for g in range(SLAB_ROWS // 4):
        at = (g // 4) * depth + (g % 4) * 3 * CASES
        tiles = [eight(y_ref, at + t * CASES) for t in range(3)]
        for i, v in enumerate(spread(*tiles)):
            rows[g * 4 + i] = halves(v)
    acc[...] = jnp.zeros_like(acc)

    def group(g, carry):
        base = g * GROUP
        wait(g)
        for first in range(0, GROUP, 8):
            terms = []
            for e in range(first, first + 8, 2):
                y = jnp.concatenate([rows[row_ref[base + e]], rows[row_ref[base + e + 1]]], axis=0)
                two = jnp.concatenate([k_ref[base + e, :BLOCK], k_ref[base + e + 1, :BLOCK]], axis=1)
                out = jnp.dot(y[:, :BLOCK], two, preferred_element_type=F32)
                terms.append(out[:8, :LANES] + out[8:16, :LANES])
                terms.append(out[16:24, LANES:] + out[24:, LANES:])
            for e in range(first, first + 8):
                j = col_ref[base + e]
                acc[j] = acc[j] + terms[e - first]
        return carry

    lax.fori_loop(0, STEPS, group, 0)
    tiles = []
    for q in range(OWN // 4):
        tiles += packed(*[acc[q * 4 + i] for i in range(4)])
    return tiles


def both_sides(core, near_ref, far_ref):
    near = [near_ref[:, tile_at(t)] for t in range(3)]
    far = [far_ref[:, tile_at(t)] for t in range(3)]
    below = [jnp.where(core == 0, f, n) for n, f in zip(near, far)]
    above = [jnp.where(core == 0, n, f) for n, f in zip(near, far)]
    return below, above


def send_sides(core, lower, upper, near_ref, far_ref):
    for t in range(3):
        near_ref[:, tile_at(t)] = jnp.where(core == 0, upper[t], lower[t])
        far_ref[:, tile_at(t)] = jnp.where(core == 0, lower[t], upper[t])


def first_product(
    col_ref, row_ref, at_ref, rhs_ref, shift_ref, diag_ref, near_ref, far_ref, k_ref,
    out_ref, inverse_ref, v_ref, near_out, far_out, held, cols, acc,
):
    core = at_ref[0]
    held[...] = jnp.zeros_like(held)
    for c in range(CASES):
        held[c : c + 1, :] = rhs_ref[c]
    below, above = both_sides(core, near_ref, far_ref)
    tiles = []
    for t in range(TILES):
        total = diag_ref[:, tile_at(t)] + shift_ref[:, tile_at(t)]
        if t < 3:
            total = total + below[t]
        if t >= 9:
            total = total + above[t - 9]
        inverse = 1.0 / total
        inverse_ref[:, tile_at(t)] = inverse
        tile = inverse * held[:, tile_at(t)]
        v_ref[:, tile_at(t)] = tile
        tiles.append(tile)
    send_sides(core, tiles[:3], tiles[9:], near_out, far_out)
    forward(col_ref, row_ref, tiles, k_ref, out_ref, cols, acc)


def image_tiles(core, tiles, v_ref, shift_ref, near_ref, far_ref):
    below, above = both_sides(core, near_ref, far_ref)
    whole = [
        tile + shift_ref[:, tile_at(t)] * v_ref[:, tile_at(t)] for t, tile in enumerate(tiles)
    ]
    return (
        [whole[t] + below[t] for t in range(3)]
        + whole[3:9]
        + [whole[t + 9] + above[t] for t in range(3)]
    )


def placed_sums(values):
    at = lane(8)
    out = jnp.zeros((8, LANES), F32)
    for n, value in values:
        out = jnp.where(at == n, jnp.sum(value, axis=1, keepdims=True), out)
    return out


def middle_product(
    col_ref, row_ref, at_ref, y_ref, shift_ref, inverse_ref, v_ref, near_ref, far_ref, k_any,
    out_ref, image_ref, w_ref, near_out, far_out, rows, cols, acc, k_ref, sems,
):
    fetch(k_any, k_ref, sems)
    core = at_ref[0]
    wait = functools.partial(fetched, k_any, k_ref, sems)
    tiles = adjoint(col_ref, row_ref, y_ref, k_ref, rows, acc, wait)
    tiles = image_tiles(core, tiles, v_ref, shift_ref, near_ref, far_ref)
    second = []
    for t, image in enumerate(tiles):
        image_ref[:, tile_at(t)] = image
        w = inverse_ref[:, tile_at(t)] * image
        w_ref[:, tile_at(t)] = w
        second.append(w)
    send_sides(core, second[:3], second[9:], near_out, far_out)
    forward(col_ref, row_ref, second, k_ref, out_ref, cols, acc)


def inner_products(rhs_ref, shift_ref, v_ref, image_ref, w_ref, sums_ref, held_ref):
    held_ref[...] = jnp.zeros_like(held_ref)
    for c in range(CASES):
        held_ref[c : c + 1, :] = rhs_ref[c]
    sums = [jnp.zeros((8, LANES), F32) for _ in range(4)]
    for t in range(TILES):
        v, w, image = (ref[:, tile_at(t)] for ref in (v_ref, w_ref, image_ref))
        sums[0] = sums[0] + held_ref[:, tile_at(t)] * v
        sums[1] = sums[1] + v * image
        sums[2] = sums[2] + image * w
        sums[3] = sums[3] + shift_ref[:, tile_at(t)] * w * w
    sums_ref[...] = placed_sums(enumerate(sums))


def last_product(
    col_ref, row_ref, at_ref, y_ref, shift_ref, v_ref, near_ref, far_ref, k_any,
    image_ref, rows, acc, k_ref, sems,
):
    fetch(k_any, k_ref, sems)
    wait = functools.partial(fetched, k_any, k_ref, sems)
    tiles = adjoint(col_ref, row_ref, y_ref, k_ref, rows, acc, wait)
    for t, tile in enumerate(image_tiles(at_ref[0], tiles, v_ref, shift_ref, near_ref, far_ref)):
        image_ref[:, tile_at(t)] = tile


def face_terms(at_ref, live_ref, near_ref, far_ref, k_ref, out_ref):
    for k, face in enumerate(both_sides(at_ref[0], near_ref, far_ref)):
        terms = []
        for i, v in enumerate(spread(*face)):
            out = lax.dot_general(
                halves(v), k_ref[k * FACE + i], (((1,), (1,)), ((), ())), preferred_element_type=F32
            )
            term = out[:8] + out[8:]
            term = jnp.where(rows_live((8, BLOCK), 1, live_ref[k], i), term, 0.0)
            terms.append(jnp.concatenate([term, jnp.zeros((8, LANES - BLOCK), F32)], axis=1))
        for t, tile in enumerate(packed(*terms)):
            out_ref[k, :, tile_at(t)] = tile


def settled(y_ref, terms_ref, *rest):
    out_ref, own_ref = rest[-2:]
    whole = y_ref[0]
    for d in range(1, y_ref.shape[0]):
        whole = whole + y_ref[d]
    own_ref[...] = whole
    for k in range(2):
        for t in range(3):
            at = (k * 9 + t) * CASES
            term = terms_ref[k, :, tile_at(t)]
            own_ref[at : at + CASES, :] = own_ref[at : at + CASES, :] + term[:CASES]
    own = own_ref[...]
    for d in range(out_ref.shape[0]):
        out_ref[d, :CHUNK] = own
    if len(rest) > 2:
        square = jnp.zeros((8, LANES), F32)
        for t in range(TILES):
            tile = eight(own_ref, t * CASES)
            square = square + tile * tile
        sums = rest[0][...] + placed_sums([(3, square)])
        for d in range(out_ref.shape[0]):
            out_ref[d, CHUNK:] = sums


def back_faces(at_ref, live_ref, own_ref, k_ref, near_out, far_out):
    backs = []
    for k in range(2):
        tiles = [eight(own_ref, (k * 9 + t) * CASES) for t in range(3)]
        terms = []
        for i, v in enumerate(spread(*tiles)):
            v = jnp.where(rows_live((8, LANES), 1, live_ref[k], i), v, 0.0)
            y = halves(v)
            out = jnp.dot(y[:, :BLOCK], k_ref[k * FACE + i], preferred_element_type=F32)
            terms.append(out[:8] + out[8:])
        backs.append(packed(*terms))
    send_sides(at_ref[0], backs[0], backs[1], near_out, far_out)


def combined(sums_ref, rhs_ref, v_ref, image_ref, w_ref, second_ref, sol_ref, res_ref):
    sums = sums_ref[0]
    for s in range(1, sums_ref.shape[0]):
        sums = sums + sums_ref[s]
    rz, curv, cross, last = (sums[:CASES, n : n + 1] for n in range(4))
    step = rz / curv
    ratio = (step * step * cross - rz) / rz
    grown = 1.0 + ratio
    curv_next = grown * grown * curv - 2.0 * grown * step * cross + step * step * last
    step_next = ratio * rz / curv_next
    on_first = step + step_next * grown
    on_second = step_next * step
    v, w = v_ref[:CASES, :], w_ref[:CASES, :]
    sol = on_first * v - on_second * w
    change = on_second * second_ref[:CASES, :] - on_first * image_ref[:CASES, :]
    for c in range(CASES):
        sol_ref[c] = sol[c : c + 1]
        res_ref[c] = rhs_ref[c : c + 1, :] + change[c : c + 1]


SMEM = pl.BlockSpec(memory_space=pltpu.SMEM)
VMEM = pl.BlockSpec(memory_space=pltpu.VMEM)


def shaped(*shape, dtype=F32):
    return jax.ShapeDtypeStruct(shape, dtype)


def in_hbm(value):
    return pltpu.with_memory_space_constraint(value, pltpu.HBM)


def call(kernel, scalars, arrays, out_shape, scratch=(), stays=0, limit=20):
    held = len(arrays) - stays
    return pl.pallas_call(
        kernel,
        in_specs=[SMEM] * len(scalars)
        + [VMEM] * held
        + [pl.BlockSpec(memory_space=pltpu.HBM)] * stays,
        out_specs=tuple(VMEM for _ in out_shape),
        out_shape=tuple(out_shape),
        scratch_shapes=list(scratch),
        compiler_params=pltpu.CompilerParams(vmem_limit_bytes=limit * MIB),
    )(*scalars, *arrays)


def body(rhs, dshift, stiff, face_k, elem_col, elem_row, face_rows):
    span = rhs.shape[2]
    face_len = FACE * BLOCK
    columns, targets = in_hbm(elem_col[0]), in_hbm(elem_row[0])
    live = in_hbm(face_rows[0])
    rhs = in_hbm(rhs.reshape(CASES, 1, span))
    dshift = in_hbm(dshift)
    core = lax.axis_index("slab_2")
    place = core.astype(jnp.int32).reshape(1)
    domains = lax.axis_size(DOM)
    slabs = lax.axis_size(SLAB)
    swap = [(0, 1), (1, 0)]
    across = [(s, (s - 1 if s % 2 == 0 else s + 1) % slabs) for s in range(slabs)]
    face = shaped(8, face_len)
    vector = shaped(8, span)

    def exchanged(near, far):
        return lax.ppermute(near, "slab_2", swap), lax.ppermute(far, SLAB, across)

    faces, face_sq = call(
        face_prep,
        [live],
        [in_hbm(face_k[0])],
        [shaped(2 * FACE, BLOCK, LANES, dtype=BF16), shaped(2, 8, face_len)],
        [pltpu.VMEM((CHUNK * 8, LANES), F32)],
    )
    sq_near, sq_far = exchanged(
        jnp.where(core == 0, face_sq[1], face_sq[0]), jnp.where(core == 0, face_sq[0], face_sq[1])
    )

    hbm = pl.BlockSpec(memory_space=pltpu.HBM)
    blocks, inner, near_blocks = pl.pallas_call(
        stiff_prep,
        in_specs=[SMEM, hbm],
        out_specs=(hbm, VMEM, VMEM),
        out_shape=(
            pltpu.HBM((STORED, BLOCK, LANES), BF16),
            vector,
            pltpu.VMEM((STORED, LANES, LANES), BF16),
        ),
        scratch_shapes=[
            pltpu.VMEM((STORED, BLOCK * BLOCK), BF16),
            pltpu.VMEM((CHUNK * PITCH, LANES), F32),
            pltpu.VMEM((OWN, 8, LANES), F32),
            pltpu.SemaphoreType.DMA((STEPS,)),
            pltpu.SemaphoreType.DMA((STEPS,)),
        ],
        compiler_params=pltpu.CompilerParams(vmem_limit_bytes=20 * MIB),
    )(columns, in_hbm(stiff[0]))
    blocks = in_hbm(blocks)
    near_blocks = pltpu.with_memory_space_constraint(near_blocks, pltpu.VMEM)

    held = pltpu.VMEM((8, span), F32)
    cols = pltpu.VMEM((OWN, 16, LANES), BF16)
    rows = pltpu.VMEM((SLAB_ROWS, 16, LANES), BF16)
    acc = pltpu.VMEM((SLAB_ROWS, 8, LANES), F32)
    stored = [pltpu.VMEM((STORED, LANES, LANES), BF16), pltpu.SemaphoreType.DMA((STEPS,))]

    def all_rows(parts, near, far, sums=()):
        near, far = exchanged(near, far)
        parts = parts.reshape(domains, CHUNK, LANES)
        arrived = lax.all_to_all(parts, DOM, 0, 0, tiled=True)
        depth = CHUNK + 8 * len(sums)
        (terms,) = call(face_terms, [place, live], [near, far, faces], [shaped(2, 8, face_len)])
        copies, own = call(
            settled,
            [],
            [arrived, terms, *sums],
            [shaped(domains, depth, LANES), shaped(CHUNK, LANES)],
        )
        full = lax.all_to_all(copies, DOM, 0, 0, tiled=True)
        near, far = call(back_faces, [place, live], [own, faces], [face, face])
        near, far = exchanged(near, far)
        return full, near, far

    parts, inverse, first, near, far = call(
        first_product,
        [columns, targets, place],
        [rhs, dshift, inner, sq_near, sq_far, near_blocks],
        [shaped(OWN * CHUNK, LANES), vector, vector, face, face],
        [held, cols, acc],
    )
    full, near, far = all_rows(parts, near, far)
    parts, image, second, near, far = call(
        middle_product,
        [columns, targets, place],
        [full.reshape(-1, LANES), dshift, inverse, first, near, far, blocks],
        [shaped(OWN * CHUNK, LANES), vector, vector, face, face],
        [rows, cols, acc, *stored],
        stays=1,
    )
    sums, whole_rhs = call(
        inner_products, [], [rhs, dshift, first, image, second], [shaped(8, LANES), vector]
    )
    full, near, far = all_rows(parts, near, far, [sums])
    full, near, far = lax.optimization_barrier((full, near, far))
    sums = jnp.sum(full[:, CHUNK:], axis=0)
    sums = lax.all_to_all(
        jnp.broadcast_to(sums[None], (slabs, *sums.shape)), SLAB, 0, 0, tiled=True
    )
    (second_image,) = call(
        last_product,
        [columns, targets, place],
        [full.reshape(-1, LANES), dshift, second, near, far, blocks],
        [vector],
        [rows, pltpu.VMEM((OWN, 8, LANES), F32), *stored],
        stays=1,
    )
    out = shaped(CASES, 1, span)
    return call(combined, [], [sums, whole_rhs, first, image, second, second_image], [out, out])


def solution(mesh):
    finer = Mesh(
        mesh.devices.reshape(4, 2, 2, 8, 2), ("slab_0", "slab_1", "slab_2", "dom_0", "dom_1")
    )
    placed = (
        P(None, SLAB, DOM),
        P(SLAB, DOM),
        P(SLAB, DOM, None),
        P(SLAB, None, DOM, None),
        P(SLAB, DOM),
        P(SLAB, DOM),
        P(SLAB, None),
    )
    return jax.shard_map(
        body,
        mesh=finer,
        in_specs=placed,
        out_specs=(P(None, SLAB, DOM), P(None, SLAB, DOM)),
        check_vma=False,
    )
```
